512 devices in a mesh: rows: 128 (over z, y, core), cols: 4 (over x).
Axes of the slice: x: 4, y: 8, z: 8, core: 2. Of those that a mesh axis runs over, the one named last changes fastest.
Arguments:
- points: bfloat16 [131072, 1024], P('rows', 'cols'), may hold values from -8 to 8
- factor: bfloat16 [131072, 1536], P('rows'), may hold values from -0.046875 to 0.046875
- targets: bfloat16 [131072, 512], P('rows', 'cols'), may hold values from -0.015625 to 0.015625
- pivot_slots: int32 [2, 1024], P(None, 'rows'), may hold values from 0 to 1023, as said below
- pivot_counts: int32 [2, 128], replicated, may hold values from 1 to 8, 256 in all within a row
Outputs:
- new_columns: float32 [2, 131072, 256], P(None, 'rows', 'cols')
- residual_diag: float32 [2, 131072], P(None, 'rows')
- coefficients: float32 [2, 256, 512], P(None, 'rows', 'cols')
The draws below stay inside these ranges and needn't reach their ends.
Inputs may be any that keep to these rules, and one draw needn't show every extreme that they name: `pivot_slots`: within one index o of rows the 8 entries of each block, and those of the two blocks together, are distinct. `pivot_counts`: each block's counts sum to 256, and the largest count of each block is 8.
All inputs are finite; a program needn't handle non-finite values.
Results may differ from the reference program's by a relative error of at most 0.0058.
Values may be sent and summed in bfloat16 or wider, within the bound.
A program may use at most 64 MiB of HBM per device.

```python
import math
import jax
import jax.numpy as jnp
import numpy as np
from jax import lax

F = 1024
K0 = 1536
NT = 512
BLOCK = 256
ROWS = 1024
NPTS = 131072
MAXP = 8
N_ROWS = 128


def draw_points(key, part):
    key = jax.random.fold_in(key, 11)
    scale_key, center_key, noise_key, member_key = jax.random.split(key, 4)
    members = jax.random.randint(member_key, (NPTS,), 0, 32).astype(jnp.int32)
    scales = jax.random.uniform(scale_key, (NPTS, 1), jnp.float32, 0.8, 1.3)
    centers = jnp.clip(jax.random.normal(center_key, (32, F), jnp.float32), -4.3, 4.3)
    noise = jnp.clip(jax.random.normal(noise_key, (NPTS, F), jnp.float32), -4.3, 4.3)
    mixed = 0.7 * jnp.take(centers, members, axis=0) + 0.7 * noise
    return jnp.clip(mixed * scales, -8.0, 8.0).astype(jnp.bfloat16)


def draw_pivot_slots(key, part):
    key = jax.random.fold_in(key, 23)
    owner_keys = jax.random.split(key, N_ROWS)
    orders = jax.vmap(lambda one_key: jax.random.permutation(one_key, ROWS))(owner_keys).astype(jnp.int32)
    marked = jax.random.randint(jax.random.fold_in(key, 5), (), 0, N_ROWS)
    top_row = ROWS - 1
    position = jnp.arange(ROWS, dtype=jnp.int32)[None, :]
    owner_ids = jnp.arange(N_ROWS, dtype=jnp.int32)[:, None]
    leading = orders[:, :1]
    swapped = jnp.where(orders == top_row, leading, jnp.where(position == 0, top_row, orders))
    orders = jnp.where(owner_ids == marked, swapped, orders)
    picked = orders[:, :2 * MAXP].reshape(N_ROWS, 2, MAXP)
    picked = jnp.transpose(picked, (1, 0, 2)).reshape(2, N_ROWS * MAXP)
    return picked.astype(jnp.int32)


def block_scale(own_key, extent, pieces, low, high):
    loudness = 1.0
    for axis_at, parts in pieces:
        steps = jax.random.uniform(jax.random.fold_in(jax.random.fold_in(own_key, 6), axis_at), (parts,), jnp.float32, low / len(pieces), high / len(pieces))
        loudness = loudness * jnp.repeat(jnp.exp(steps), extent[axis_at] // parts).reshape((-1,) + (1,) * (len(extent) - 1 - axis_at))
    return loudness


def length_profile(count, total, bound, lean):
    loads = [(1 << 20) // math.isqrt(grade ** lean) + 1 for grade in range(2, count + 1)]
    rest, given = total - bound - (count - 1), [1] * (count - 1)
    while rest > 0:
        candidates = [i for i in range(count - 1) if given[i] < bound]
        mass, left = sum([loads[i] for i in candidates]), rest
        for i in candidates:
            addition = min(bound - given[i], max(1, left * loads[i] // mass), rest)
            given[i] = given[i] + addition
            rest = rest - addition
    return np.array([bound] + given)


def ragged_sizes(stream_key, count, total, limit, skew):
    if count == 2:
        one = jax.random.randint(stream_key, (), max(1, total - limit), min(limit, total - 1) + 1)
        return jnp.stack([one, total - one])
    lengths = jnp.asarray(length_profile(count, total, limit, skew), jnp.int32)
    couples = (count - 1) // 2
    donor, receiver = lengths[1:1 + 2 * couples:2], lengths[2:2 + 2 * couples:2]
    margin = jnp.minimum(donor - 1, limit - receiver)
    passed = jax.random.randint(jax.random.fold_in(stream_key, 1), (couples,), 0, 1 << 20) % (margin + 1)
    lengths = lengths.at[1:1 + 2 * couples:2].set(donor - passed).at[2:2 + 2 * couples:2].set(receiver + passed)
    return lengths[jax.random.permutation(jax.random.fold_in(stream_key, 2), count)]


def normal_values(key, shape, spread, reach, shards=(), kind=jnp.bfloat16):
    entries = spread * jax.random.normal(key, shape, jnp.float32)
    if shards:
        entries = entries * block_scale(key, shape, shards, -0.22, 0.18)
    return jnp.clip(entries, -reach, reach).astype(kind)


def setup_inputs(seed: int = 0) -> dict:
    keys = jax.random.split(jax.random.key(seed), 6)
    return {
        "points": draw_points(jax.random.fold_in(keys[5], 71), 0),
        "factor": normal_values(keys[1], (NPTS, K0), (8 * (K0 + 2 * BLOCK)) ** -0.5, 0.046875, ((0, 128),)),
        "targets": normal_values(keys[2], (NPTS, NT), NPTS ** -0.5, 0.015625, ((0, 128), (1, 4))),
        "pivot_slots": draw_pivot_slots(jax.random.fold_in(keys[5], 71), 0),
        "pivot_counts": jax.vmap(lambda own: ragged_sizes(own, N_ROWS, BLOCK, MAXP, 2))(jax.random.split(keys[4], 2)).reshape((2, N_ROWS)).astype(jnp.int32),
    }


def place_pivots(counts):
    inclusive = jnp.cumsum(counts).astype(jnp.int32)
    exclusive = inclusive - counts
    pick_index = jnp.arange(BLOCK, dtype=jnp.int32)
    owners = jnp.sum((inclusive[None, :] <= pick_index[:, None]).astype(jnp.int32), axis=1, dtype=jnp.int32)
    owner_ids = jnp.arange(counts.shape[0], dtype=jnp.int32)
    starts = jnp.sum(jnp.where(owner_ids[None, :] == owners[:, None], exclusive[None, :], 0), axis=1, dtype=jnp.int32)
    return (owners, (pick_index - starts).astype(jnp.int32))

def cross_rows(left, right):
    return lax.dot_general(left.astype(jnp.float32), right.astype(jnp.float32), (((1,), (1,)), ((), ())), preferred_element_type=jnp.float32)

def reference(points, factor, targets, pivot_slots, pivot_counts):
    sq_norm = jnp.sum(jnp.square(points.astype(jnp.float32)), axis=1)
    current = factor
    residual = 1.0 - jnp.sum(jnp.square(factor.astype(jnp.float32)), axis=1)
    outputs_new = []
    outputs_res = []
    outputs_coeff = []
    for section_index in range(2):
        owners, slot_pos = place_pivots(pivot_counts[section_index])
        local_rows = jnp.take(pivot_slots[section_index], (owners * MAXP + slot_pos).astype(jnp.int32))
        pivots = (owners * ROWS + local_rows).astype(jnp.int32)
        chosen = jnp.take(points, pivots, axis=0)
        distance = sq_norm[:, None] + jnp.take(sq_norm, pivots)[None, :] - 2.0 * cross_rows(points, chosen)
        columns = jnp.exp(-distance / F) - cross_rows(current, jnp.take(current, pivots, axis=0))
        pivot_block = jnp.take(columns, pivots, axis=0)
        cholesky_low = jnp.linalg.cholesky(pivot_block)
        fresh_cols = jax.scipy.linalg.solve_triangular(cholesky_low, columns.T, lower=True).T
        narrow = fresh_cols.astype(jnp.bfloat16)
        residual = residual - jnp.sum(jnp.square(fresh_cols), axis=1)
        coeff_full = lax.dot_general(narrow.astype(jnp.float32), targets.astype(jnp.float32), (((0,), (0,)), ((), ())), preferred_element_type=jnp.float32)
        outputs_new.append(fresh_cols)
        outputs_res.append(residual)
        outputs_coeff.append(coeff_full)
        current = jnp.concatenate([current, narrow], axis=1)
    return (jnp.stack(outputs_new, axis=0), jnp.stack(outputs_res, axis=0), jnp.stack(outputs_coeff, axis=0))
```

```python
import functools
import jax
import jax.numpy as jnp
from jax import lax
from jax.experimental import pallas as pl
from jax.experimental.pallas import tpu as pltpu
from jax.sharding import PartitionSpec as P

F = 1024
BLOCK = 256
MAXP = 8
NX = 4
FQ = 256
KQ = 384
W = FQ + KQ
ROWS = 1024
TILE = 256
HI = lax.Precision.HIGHEST
f32 = jnp.float32
bf16 = jnp.bfloat16


def mm_nt(a, b, precision=None):
    return lax.dot_general(
        a, b, (((1,), (1,)), ((), ())), precision=precision, preferred_element_type=f32
    )


def mm_nn(a, b, precision=None):
    return lax.dot_general(
        a, b, (((1,), (0,)), ((), ())), precision=precision, preferred_element_type=f32
    )


def mm_tn(a, b):
    return lax.dot_general(a, b, (((0,), (0,)), ((), ())), preferred_element_type=f32)


def split2(a):
    high = a.astype(bf16)
    return high, (a - high.astype(f32)).astype(bf16)


def chol_inv_128(a):
    n = 16
    sub = lax.broadcasted_iota(jnp.int32, (8, 128), 0)
    lane = lax.broadcasted_iota(jnp.int32, (8, 128), 1)
    A = [a[8 * r : 8 * r + 8, :] for r in range(n)]
    X = [jnp.where(lane == sub + 8 * r, 1.0, 0.0).astype(f32) for r in range(n)]
    out = []
    for k in range(n):
        panel = [
            [jnp.broadcast_to(A[r][:, 8 * k + m : 8 * k + m + 1], (8, 128)) for m in range(8)]
            if r >= k
            else None
            for r in range(n)
        ]
        pivots = jnp.ones((8, 128), f32)
        for j in range(8):
            row = lambda v: jnp.broadcast_to(v[j : j + 1, :], (8, 128))
            row_a, row_x = row(A[k]), row(X[k])
            row_p = [row(panel[k][m]) if m >= j else None for m in range(8)]
            pivots = jnp.where(sub == j, row_p[j], pivots)
            inverse = 1.0 / row_p[j]
            for r in range(k, n):
                c = panel[r][j] * inverse
                if r == k:
                    if j == 7:
                        continue
                    c = jnp.where(sub > j, c, 0.0)
                A[r] = A[r] - c * row_a
                X[r] = X[r] - c * row_x
                for m in range(j + 1, 8):
                    panel[r][m] = panel[r][m] - c * row_p[m]
        out.append(X[k] * lax.rsqrt(pivots))
    return jnp.concatenate(out, axis=0)


def chol_inv_256(a):
    inv11 = chol_inv_128(a[:128, :128])
    low21 = mm_nt(a[128:, :128], inv11, HI)
    inv22 = chol_inv_128(a[128:, 128:] - mm_nt(low21, low21, HI))
    inv21 = -mm_nn(inv22, mm_nn(low21, inv11, HI), HI)
    zero = jnp.zeros((128, 128), f32)
    return jnp.concatenate(
        [jnp.concatenate([inv11, zero], axis=1), jnp.concatenate([inv21, inv22], axis=1)], axis=0
    )


def factor_kernel(g_ref, inv_ref, cross_ref, sq_ref):
    def gram(a, b):
        ra, rb = slice(256 * a, 256 * a + 256), slice(256 * b, 256 * b + 256)
        dots = sum(mm_nt(g_ref[c, ra, :FQ], g_ref[c, rb, :FQ]) for c in range(NX))
        basis = sum(mm_nt(g_ref[c, ra, FQ:], g_ref[c, rb, FQ:]) for c in range(NX))
        return dots, basis

    eye = lax.broadcasted_iota(jnp.int32, (256, 256), 0) == lax.broadcasted_iota(
        jnp.int32, (256, 256), 1
    )

    def norms(dots):
        diag = jnp.where(eye, dots, 0.0)
        return jnp.sum(diag, axis=1, keepdims=True), jnp.sum(diag, axis=0, keepdims=True)

    dots00, basis00 = gram(0, 0)
    dots10, basis10 = gram(1, 0)
    dots11, basis11 = gram(1, 1)
    col0, row0 = norms(dots00)
    col1, row1 = norms(dots11)
    sq_ref[:, :256] = jnp.broadcast_to(row0, (8, 256))
    sq_ref[:, 256:] = jnp.broadcast_to(row1, (8, 256))
    a00 = jnp.exp(-(col0 + row0 - 2.0 * dots00) / F) - basis00
    a10 = jnp.exp(-(col1 + row0 - 2.0 * dots10) / F) - basis10
    a11 = jnp.exp(-(col1 + row1 - 2.0 * dots11) / F) - basis11
    inv0 = chol_inv_256(a00)
    narrow10 = mm_nt(a10, inv0, HI).astype(bf16)
    inv1 = chol_inv_256(a11 - mm_nt(narrow10, narrow10))
    cross_ref[...] = narrow10
    inv_ref[0, 0], inv_ref[0, 1] = split2(inv0)
    inv_ref[1, 0], inv_ref[1, 1] = split2(inv1)


def factor_pivots(g):
    return pl.pallas_call(
        factor_kernel,
        out_shape=(
            jax.ShapeDtypeStruct((2, 2, BLOCK, BLOCK), bf16),
            jax.ShapeDtypeStruct((BLOCK, BLOCK), bf16),
            jax.ShapeDtypeStruct((8, 2 * BLOCK), f32),
        ),
        compiler_params=pltpu.CompilerParams(vmem_limit_bytes=40 * 2**20),
        cost_estimate=pl.CostEstimate(
            flops=60_000_000_000, bytes_accessed=4_000_000, transcendentals=0
        ),
        name="pivot_factor",
    )(g)


def fold(v):
    total = v[:, :128]
    for i in range(1, v.shape[1] // 128):
        total = total + v[:, 128 * i : 128 * i + 128]
    return total


def rows_kernel(place_ref, x_ref, f_ref, t_ref, g_ref, inv_ref, cross_ref, sq_ref, new_ref, res_ref, coef_ref):
    place = place_ref[0]
    dots = jnp.zeros((TILE, 512), f32)
    basis = jnp.zeros((TILE, 512), f32)
    squares = jnp.zeros((TILE, 128), f32)
    factor_squares = jnp.zeros((TILE, 128), f32)
    for c in range(NX):
        x = x_ref[c]
        fac = f_ref[:, KQ * c : KQ * c + KQ]
        dots = dots + mm_nt(x, g_ref[c, :, :FQ])
        basis = basis + mm_nt(fac, g_ref[c, :, FQ:])
        squares = squares + fold(jnp.square(x.astype(f32)))
        factor_squares = factor_squares + fold(jnp.square(fac.astype(f32)))
    sq = jnp.sum(squares, axis=1, keepdims=True)
    columns = jnp.exp(-(sq + sq_ref[0:1, :] - 2.0 * dots) / F) - basis

    def solve(b, cols):
        high, low = split2(cols)
        return (
            mm_nt(high, inv_ref[b, 0]) + mm_nt(high, inv_ref[b, 1]) + mm_nt(low, inv_ref[b, 0])
        )

    def keep(b, fresh):
        half = jnp.where(place >= 2, fresh[:, 128:], fresh[:, :128])
        part = jnp.where(place % 2 == 1, pltpu.roll(half, 64, 1), half)
        new_ref[b] = part[:, :64]

    def across(v):
        return jnp.sum(jnp.transpose(v), axis=0, keepdims=True)

    @pl.when(pl.program_id(0) == 0)
    def _():
        coef_ref[...] = jnp.zeros_like(coef_ref)

    fresh0 = solve(0, columns[:, :256])
    narrow0 = fresh0.astype(bf16)
    fresh1 = solve(1, columns[:, 256:] - mm_nt(narrow0, cross_ref[...]))
    narrow1 = fresh1.astype(bf16)
    keep(0, fresh0)
    keep(1, fresh1)
    res0 = 1.0 - across(factor_squares + fold(jnp.square(fresh0)))
    res_ref[0:1, :] = res0
    res_ref[1:2, :] = res0 - across(fold(jnp.square(fresh1)))
    coef_ref[:256] += mm_tn(narrow0, t_ref[...])
    coef_ref[256:] += mm_tn(narrow1, t_ref[...])


def solve_rows(place, x, factor, targets, g, inv, cross, sq):
    whole = lambda shape: pl.BlockSpec(shape, lambda i: (0,) * len(shape))
    return pl.pallas_call(
        rows_kernel,
        grid=(ROWS // TILE,),
        in_specs=[
            pl.BlockSpec(memory_space=pltpu.SMEM),
            pl.BlockSpec((NX, TILE, FQ), lambda i: (0, i, 0)),
            pl.BlockSpec((TILE, NX * KQ), lambda i: (i, 0)),
            pl.BlockSpec((TILE, 128), lambda i: (i, 0)),
            whole((NX, 512, W)),
            whole((2, 2, BLOCK, BLOCK)),
            whole((BLOCK, BLOCK)),
            whole((8, 512)),
        ],
        out_specs=[
            pl.BlockSpec((2, TILE, 64), lambda i: (0, i, 0)),
            pl.BlockSpec((2, TILE), lambda i: (0, i)),
            whole((512, 128)),
        ],
        out_shape=(
            jax.ShapeDtypeStruct((2, ROWS, 64), f32),
            jax.ShapeDtypeStruct((2, ROWS), f32),
            jax.ShapeDtypeStruct((512, 128), f32),
        ),
        compiler_params=pltpu.CompilerParams(vmem_limit_bytes=40 * 2**20),
        name="row_solve",
    )(place, x, factor, targets, g, inv, cross, sq)


def place_pivots(counts):
    inclusive = jnp.cumsum(counts)
    exclusive = inclusive - counts
    pick_index = jnp.arange(BLOCK, dtype=jnp.int32)
    owners = jnp.sum(
        (inclusive[None, :] <= pick_index[:, None]).astype(jnp.int32), axis=1, dtype=jnp.int32
    )
    owner_ids = jnp.arange(counts.shape[0], dtype=jnp.int32)
    starts = jnp.sum(
        jnp.where(owner_ids[None, :] == owners[:, None], exclusive[None, :], 0),
        axis=1,
        dtype=jnp.int32,
    )
    return owners, pick_index - starts


def local(points, factor, targets, pivot_slots, pivot_counts):
    place = lax.axis_index("cols")
    quarter = lax.dynamic_slice_in_dim(factor, place * KQ, KQ, 1)
    rows = pivot_slots.reshape(2 * MAXP)
    slots = jnp.concatenate([points[rows], quarter[rows]], axis=1)
    gathered = lax.all_gather(slots, "rows", axis=0, tiled=False)
    picks = []
    for b in range(2):
        owners, slot = place_pivots(pivot_counts[b])
        picks.append(owners * 2 * MAXP + b * MAXP + slot)
    chosen = jnp.take(gathered.reshape(-1, W), jnp.concatenate(picks), axis=0)
    g = lax.all_gather(chosen, "cols", axis=0, tiled=False)
    x = lax.all_gather(points, "cols", axis=0, tiled=False)
    inv, cross, sq = factor_pivots(g)
    new, res, coef = solve_rows(
        place.reshape(1).astype(jnp.int32), x, factor, targets, g, inv, cross, sq
    )
    coef = lax.psum_scatter(
        coef.reshape(2, BLOCK, 128), "rows", scatter_dimension=1, tiled=True
    )
    return new, res, coef


def solution(mesh):
    in_specs = (P("rows", "cols"), P("rows", None), P("rows", "cols"), P(None, "rows"), P())
    out_specs = (P(None, "rows", "cols"), P(None, "rows"), P(None, "rows", "cols"))
    return jax.shard_map(local, mesh=mesh, in_specs=in_specs, out_specs=out_specs, check_vma=False)
```

```python
import functools
import jax
import jax.numpy as jnp
from jax import lax
from jax.experimental import pallas as pl
from jax.experimental.pallas import tpu as pltpu
from jax.sharding import PartitionSpec as P

F = 1024
BLOCK = 256
MAXP = 8
NX = 4
FQ = 256
KQ = 384
W = FQ + KQ
ROWS = 1024
TILE = 256
HI = lax.Precision.HIGHEST
f32 = jnp.float32
bf16 = jnp.bfloat16


def mm_nt(a, b, precision=None):
    return lax.dot_general(
        a, b, (((1,), (1,)), ((), ())), precision=precision, preferred_element_type=f32
    )


def mm_nn(a, b, precision=None):
    return lax.dot_general(
        a, b, (((1,), (0,)), ((), ())), precision=precision, preferred_element_type=f32
    )


def mm_tn(a, b):
    return lax.dot_general(a, b, (((0,), (0,)), ((), ())), preferred_element_type=f32)


def split2(a):
    high = a.astype(bf16)
    return high, (a - high.astype(f32)).astype(bf16)


def chol_inv_128(a):
    n = 16
    sub = lax.broadcasted_iota(jnp.int32, (8, 128), 0)
    lane = lax.broadcasted_iota(jnp.int32, (8, 128), 1)
    A = [a[8 * r : 8 * r + 8, :] for r in range(n)]
    X = [jnp.where(lane == sub + 8 * r, 1.0, 0.0).astype(f32) for r in range(n)]
    out = []
    for k in range(n):
        panel = [
            [jnp.broadcast_to(A[r][:, 8 * k + m : 8 * k + m + 1], (8, 128)) for m in range(8)]
            if r >= k
            else None
            for r in range(n)
        ]
        pivots = jnp.ones((8, 128), f32)
        for j in range(8):
            row = lambda v: jnp.broadcast_to(v[j : j + 1, :], (8, 128))
            row_a, row_x = row(A[k]), row(X[k])
            row_p = [row(panel[k][m]) if m >= j else None for m in range(8)]
            pivots = jnp.where(sub == j, row_p[j], pivots)
            inverse = 1.0 / row_p[j]
            for r in range(k, n):
                c = panel[r][j] * inverse
                if r == k:
                    if j == 7:
                        continue
                    c = jnp.where(sub > j, c, 0.0)
                A[r] = A[r] - c * row_a
                X[r] = X[r] - c * row_x
                for m in range(j + 1, 8):
                    panel[r][m] = panel[r][m] - c * row_p[m]
        out.append(X[k] * lax.rsqrt(pivots))
    return jnp.concatenate(out, axis=0)


def chol_inv_256(a):
    inv11 = chol_inv_128(a[:128, :128])
    low21 = mm_nt(a[128:, :128], inv11, HI)
    inv22 = chol_inv_128(a[128:, 128:] - mm_nt(low21, low21, HI))
    inv21 = -mm_nn(inv22, mm_nn(low21, inv11, HI), HI)
    zero = jnp.zeros((128, 128), f32)
    return jnp.concatenate(
        [jnp.concatenate([inv11, zero], axis=1), jnp.concatenate([inv21, inv22], axis=1)], axis=0
    )


def factor_kernel(g_ref, inv_ref, cross_ref, sq_ref):
    def gram(a, b):
        dots = sum(mm_nt(g_ref[c, a, :, :FQ], g_ref[c, b, :, :FQ]) for c in range(NX))
        basis = sum(mm_nt(g_ref[c, a, :, FQ:], g_ref[c, b, :, FQ:]) for c in range(NX))
        return dots, basis

    eye = lax.broadcasted_iota(jnp.int32, (256, 256), 0) == lax.broadcasted_iota(
        jnp.int32, (256, 256), 1
    )

    def norms(dots):
        diag = jnp.where(eye, dots, 0.0)
        return jnp.sum(diag, axis=1, keepdims=True), jnp.sum(diag, axis=0, keepdims=True)

    dots00, basis00 = gram(0, 0)
    dots10, basis10 = gram(1, 0)
    dots11, basis11 = gram(1, 1)
    col0, row0 = norms(dots00)
    col1, row1 = norms(dots11)
    sq_ref[:, :256] = jnp.broadcast_to(row0, (8, 256))
    sq_ref[:, 256:] = jnp.broadcast_to(row1, (8, 256))
    a00 = jnp.exp(-(col0 + row0 - 2.0 * dots00) / F) - basis00
    a10 = jnp.exp(-(col1 + row0 - 2.0 * dots10) / F) - basis10
    a11 = jnp.exp(-(col1 + row1 - 2.0 * dots11) / F) - basis11
    inv0 = chol_inv_256(a00)
    narrow10 = mm_nt(a10, inv0, HI).astype(bf16)
    inv1 = chol_inv_256(a11 - mm_nt(narrow10, narrow10))
    cross_ref[...] = narrow10
    inv_ref[0, 0], inv_ref[0, 1] = split2(inv0)
    inv_ref[1, 0], inv_ref[1, 1] = split2(inv1)


def factor_pivots(g):
    return pl.pallas_call(
        factor_kernel,
        out_shape=(
            jax.ShapeDtypeStruct((2, 2, BLOCK, BLOCK), bf16),
            jax.ShapeDtypeStruct((BLOCK, BLOCK), bf16),
            jax.ShapeDtypeStruct((8, 2 * BLOCK), f32),
        ),
        compiler_params=pltpu.CompilerParams(vmem_limit_bytes=40 * 2**20),
        cost_estimate=pl.CostEstimate(
            flops=60_000_000_000, bytes_accessed=4_000_000, transcendentals=0
        ),
        name="pivot_factor",
    )(g)


def fold(v):
    total = v[:, :128]
    for i in range(1, v.shape[1] // 128):
        total = total + v[:, 128 * i : 128 * i + 128]
    return total


def rows_kernel(
    x0_ref, x1_ref, x2_ref, x3_ref, f_ref, t_ref, g_ref, inv_ref, cross_ref, sq_ref,
    new_ref, res_ref, coef_ref,
):
    place = lax.axis_index("cols")
    dots = jnp.zeros((TILE, 512), f32)
    basis = jnp.zeros((TILE, 512), f32)
    squares = jnp.zeros((TILE, 128), f32)
    factor_squares = jnp.zeros((TILE, 128), f32)
    for c, x_ref in enumerate((x0_ref, x1_ref, x2_ref, x3_ref)):
        x = x_ref[...]
        fac = f_ref[:, KQ * c : KQ * c + KQ]
        dots = dots + mm_nt(x, g_ref[(place + c) % NX, :, :, :FQ].reshape(512, FQ))
        basis = basis + mm_nt(fac, g_ref[c, :, :, FQ:].reshape(512, KQ))
        squares = squares + fold(jnp.square(x.astype(f32)))
        factor_squares = factor_squares + fold(jnp.square(fac.astype(f32)))
    sq = jnp.sum(squares, axis=1, keepdims=True)
    columns = jnp.exp(-(sq + sq_ref[0:1, :] - 2.0 * dots) / F) - basis

    def solve(b, cols):
        high, low = split2(cols)
        return (
            mm_nt(high, inv_ref[b, 0]) + mm_nt(high, inv_ref[b, 1]) + mm_nt(low, inv_ref[b, 0])
        )

    def keep(b, fresh):
        half = jnp.where(place >= 2, fresh[:, 128:], fresh[:, :128])
        part = jnp.where(place % 2 == 1, pltpu.roll(half, 64, 1), half)
        new_ref[b] = part[:, :64]

    def across(v):
        return jnp.sum(jnp.transpose(v), axis=0, keepdims=True)

    @pl.when(pl.program_id(0) == 0)
    def _():
        coef_ref[...] = jnp.zeros_like(coef_ref)

    fresh0 = solve(0, columns[:, :256])
    narrow0 = fresh0.astype(bf16)
    fresh1 = solve(1, columns[:, 256:] - mm_nt(narrow0, cross_ref[...]))
    narrow1 = fresh1.astype(bf16)
    keep(0, fresh0)
    keep(1, fresh1)
    res0 = 1.0 - across(factor_squares + fold(jnp.square(fresh0)))
    res_ref[0:1, :] = res0
    res_ref[1:2, :] = res0 - across(fold(jnp.square(fresh1)))
    coef_ref[0] += mm_tn(narrow0, t_ref[...])
    coef_ref[1] += mm_tn(narrow1, t_ref[...])


def solve_rows(xs, factor, targets, g, inv, cross, sq):
    whole = lambda shape: pl.BlockSpec(shape, lambda i: (0,) * len(shape))
    return pl.pallas_call(
        rows_kernel,
        grid=(ROWS // TILE,),
        in_specs=[
            *[pl.BlockSpec((TILE, FQ), lambda i: (i, 0))] * NX,
            pl.BlockSpec((TILE, NX * KQ), lambda i: (i, 0)),
            pl.BlockSpec((TILE, 128), lambda i: (i, 0)),
            whole((NX, 2, BLOCK, W)),
            whole((2, 2, BLOCK, BLOCK)),
            whole((BLOCK, BLOCK)),
            whole((8, 512)),
        ],
        out_specs=[
            pl.BlockSpec((2, TILE, 64), lambda i: (0, i, 0)),
            pl.BlockSpec((2, TILE), lambda i: (0, i)),
            whole((2, BLOCK, 128)),
        ],
        out_shape=(
            jax.ShapeDtypeStruct((2, ROWS, 64), f32),
            jax.ShapeDtypeStruct((2, ROWS), f32),
            jax.ShapeDtypeStruct((2, BLOCK, 128), f32),
        ),
        compiler_params=pltpu.CompilerParams(vmem_limit_bytes=40 * 2**20),
        name="row_solve",
    )(*xs, factor, targets, g, inv, cross, sq)

NZ = 8
NY = 8
CORES = 2
MESH = pl.DeviceIdType.MESH


def spot():
    index = lax.axis_index("rows")
    return index // (NY * CORES), (index // CORES) % NY, index % CORES


def row_id(z, y, core):
    return {"rows": (z * NY + y) * CORES + core}


def enter(devices):
    barrier = pltpu.get_barrier_semaphore()
    for device in devices:
        pl.semaphore_signal(barrier, inc=1, device_id=device, device_id_type=MESH)
    return lambda: pl.semaphore_wait(barrier, len(devices))


def remote(src, dst, sems, index, device):
    return pltpu.make_async_remote_copy(
        src_ref=src,
        dst_ref=dst,
        send_sem=sems.at[0, index],
        recv_sem=sems.at[1, index],
        device_id=device,
        device_id_type=MESH,
    )


def gather_kernel(
    slots_ref, counts_ref, points_ref, factor_ref, g_ref,
    quarter, own, other, buf_a, buf_b, load_sem,
    core_sem, ya_sem, zb_sem, za_sem, yb_sem, x_sem, k_sem,
):
    z, y, core = spot()
    x = lax.axis_index("cols")
    sibling = row_id(z, y, 1 - core)
    y_peers = [row_id(z, (y + d) % NY, core) for d in range(1, NY)]
    z_peers = [row_id((z + d) % NZ, y, core) for d in range(1, NZ)]
    right, left = {"cols": (x + 1) % NX}, {"cols": (x + NX - 1) % NX}
    load = pltpu.make_async_copy(
        factor_ref.at[:, pl.ds(pl.multiple_of(x * KQ, 128), KQ)], quarter, load_sem
    )
    load.start()
    wait_entered = enter([sibling] + y_peers + z_peers + [right, left])

    slots = slots_ref[:, 0:1]
    chosen = (lax.broadcasted_iota(jnp.int32, (2 * MAXP, ROWS), 1) == slots).astype(bf16)
    own[:, :FQ] = mm_nn(chosen, points_ref[...]).astype(bf16)
    load.wait()
    own[:, FQ:] = mm_nn(chosen, quarter[...]).astype(bf16)
    wait_entered()

    swap = remote(own, other, core_sem, 0, sibling)
    swap.start()
    swap.wait()
    mine, theirs = own[...].astype(f32), other[...].astype(f32)
    first = core == 0
    pair = jnp.concatenate(
        [
            jnp.where(first, mine[:MAXP], theirs[MAXP:]),
            jnp.where(first, theirs[:MAXP], mine[MAXP:]),
        ],
        axis=0,
    ).astype(bf16)
    buf_a[z, y] = pair[:, FQ:]
    buf_b[y, z] = pair[:, :FQ]
    along_y = [
        remote(buf_a.at[z, y], buf_a.at[z, y], ya_sem, d, y_peers[d]) for d in range(NY - 1)
    ]
    along_z = [
        remote(buf_b.at[y, z], buf_b.at[y, z], zb_sem, d, z_peers[d]) for d in range(NZ - 1)
    ]
    for one, two in zip(along_y, along_z):
        one.start()
        two.start()

    counts = jnp.where(first, counts_ref[0:1, :], counts_ref[1:2, :]).astype(f32)
    counts = jnp.broadcast_to(counts, (8, 128)).astype(bf16)
    before = lax.broadcasted_iota(jnp.int32, (128, 128), 0) < lax.broadcasted_iota(
        jnp.int32, (128, 128), 1
    )
    offsets = mm_nn(counts, before.astype(bf16)).astype(bf16)
    owner_row = lax.broadcasted_iota(jnp.int32, (128, 1024), 0)
    column = lax.broadcasted_iota(jnp.int32, (128, 1024), 1)
    slot = (lax.broadcasted_iota(jnp.int32, (8, 1024), 1) % MAXP).astype(f32)
    pivot_row = lax.broadcasted_iota(jnp.int32, (BLOCK, 1024), 0)

    def places(owner_of):
        spread = (owner_row == owner_of(column // MAXP)).astype(bf16)
        start, count = mm_nn(offsets, spread), mm_nn(counts, spread)
        target = jnp.where(slot < count, start + slot, -1.0)
        return (pivot_row.astype(f32) == target[0:1, :]).astype(bf16)

    def swapped(position):
        return ((position // CORES) % NZ * NY + position // (CORES * NZ)) * CORES + position % CORES

    compact_a = places(lambda position: position)
    compact_b = places(swapped)

    for d in range(NY - 1):
        source = (y + NY - 1 - d) % NY
        remote(buf_a.at[z, source], buf_a.at[z, source], ya_sem, d, y_peers[d]).wait_recv()
    for d in range(NZ - 1):
        source = (z + NZ - 1 - d) % NZ
        remote(buf_b.at[y, source], buf_b.at[y, source], zb_sem, d, z_peers[d]).wait_recv()

    def ring(buf, sems, me, count, up, down):
        ahead, back = count // 2, (count - 1) // 2

        def send(step):
            if step < ahead:
                part = buf.at[(me + count - step) % count]
                remote(part, part, sems, step, up).start()
            if step < back:
                part = buf.at[(me + step) % count]
                remote(part, part, sems, ahead + step, down).start()

        def receive(step):
            if step < ahead:
                part = buf.at[(me + count - 1 - step) % count]
                remote(part, part, sems, step, up).wait_recv()
            if step < back:
                part = buf.at[(me + 1 + step) % count]
                remote(part, part, sems, ahead + step, down).wait_recv()

        def finish():
            for step in range(ahead + back):
                remote(buf.at[0], buf.at[0], sems, step, up).wait_send()

        return send, receive, finish, ahead

    send_a, receive_a, finish_a, steps = ring(buf_a, za_sem, z, NZ, z_peers[0], z_peers[NZ - 2])
    send_b, receive_b, finish_b, _ = ring(buf_b, yb_sem, y, NY, y_peers[0], y_peers[NY - 2])
    for step in range(steps):
        send_a(step)
        send_b(step)
        receive_a(step)
        receive_b(step)

    g_ref[x, core, :, FQ:] = mm_nn(compact_a, buf_a[...].reshape(1024, KQ)).astype(bf16)
    g_ref[x, core, :, :FQ] = mm_nn(compact_b, buf_b[...].reshape(1024, FQ)).astype(bf16)

    half = BLOCK // 2
    x_left, x_right, x_far = (x + NX - 1) % NX, (x + 1) % NX, (x + 2) % NX

    def part(origin, at):
        return g_ref.at[origin, core, pl.ds(at * half, half), :]

    def to_right(origin, at, index):
        return remote(part(origin, at), part(origin, at), x_sem, index, right)

    def to_left(origin, at, index):
        return remote(part(origin, at), part(origin, at), x_sem, 3 + index, left)

    def to_sibling(origin):
        return remote(g_ref.at[origin, core], g_ref.at[origin, core], k_sem, origin, sibling)

    sends = [to_right(x, 0, 0), to_left(x, 1, 0), to_right(x, 1, 1), to_left(x, 0, 1), to_sibling(x)]
    for copy in sends:
        copy.start()
    to_right(x_left, 0, 0).wait_recv()
    sends.append(to_right(x_left, 0, 2))
    sends[-1].start()
    to_left(x_right, 1, 0).wait_recv()
    sends.append(to_left(x_right, 1, 2))
    sends[-1].start()
    to_right(x_left, 1, 1).wait_recv()
    sends.append(to_sibling(x_left))
    sends[-1].start()
    to_left(x_right, 0, 1).wait_recv()
    sends.append(to_sibling(x_right))
    sends[-1].start()
    to_right(x_far, 0, 2).wait_recv()
    to_left(x_far, 1, 2).wait_recv()
    sends.append(to_sibling(x_far))
    sends[-1].start()
    for origin in range(NX):
        arrived = g_ref.at[origin, 1 - core]
        remote(arrived, arrived, k_sem, origin, sibling).wait_recv()
    for copy in along_y + along_z + sends:
        copy.wait_send()
    finish_a()
    finish_b()


def gather_pivots(slots, counts, points, factor):
    vmem = pl.BlockSpec(memory_space=pltpu.VMEM)
    sems = lambda count: pltpu.SemaphoreType.DMA((2, count))
    return pl.pallas_call(
        gather_kernel,
        in_specs=[vmem, vmem, vmem, pl.BlockSpec(memory_space=pl.ANY)],
        out_specs=vmem,
        out_shape=jax.ShapeDtypeStruct((NX, 2, BLOCK, W), bf16),
        scratch_shapes=[
            pltpu.VMEM((ROWS, KQ), bf16),
            pltpu.VMEM((2 * MAXP, W), bf16),
            pltpu.VMEM((2 * MAXP, W), bf16),
            pltpu.VMEM((NZ, NY, 2 * MAXP, KQ), bf16),
            pltpu.VMEM((NY, NZ, 2 * MAXP, FQ), bf16),
            pltpu.SemaphoreType.DMA,
            sems(1),
            sems(NY - 1),
            sems(NZ - 1),
            sems(NZ - 1),
            sems(NY - 1),
            sems(6),
            sems(NX),
        ],
        compiler_params=pltpu.CompilerParams(
            collective_id=0, has_side_effects=True, vmem_limit_bytes=40 * 2**20
        ),
        name="pivot_gather",
    )(slots, counts, points, factor)


def sum_kernel(coef_ref, out_ref, got, total, got_z, piece, got_y, final, core_sem, z_sem, y_sem, k_sem):
    z, y, core = spot()
    sibling = row_id(z, y, 1 - core)
    y_peers = [row_id(z, (y + d) % NY, core) for d in range(1, NY)]
    z_peers = [row_id((z + d) % NZ, y, core) for d in range(1, NZ)]
    enter([sibling] + y_peers + z_peers)()

    swap = remote(coef_ref.at[1 - core], got, core_sem, 0, sibling)
    swap.start()
    swap.wait()
    total[...] = (coef_ref[core] + got[...]).reshape(NZ, 32, 128)
    over_z = [
        remote(total.at[(z + d + 1) % NZ], got_z.at[d], z_sem, d, z_peers[d])
        for d in range(NZ - 1)
    ]
    for copy in over_z:
        copy.start()
    for copy in over_z:
        copy.wait()
    mine = total[z]
    for d in range(NZ - 1):
        mine = mine + got_z[d]
    piece[...] = mine.reshape(4, 8, 128)
    over_y = [
        remote(piece.at[(y + d + 1) % NY // 2], got_y.at[d], y_sem, d, y_peers[d])
        for d in range(NY - 1)
    ]
    for copy in over_y:
        copy.start()
    for copy in over_y:
        copy.wait()
    mine = piece[y // 2]
    for d in range(NY - 1):
        mine = mine + got_y[d]
    final[core] = mine
    last = remote(final.at[core], final.at[core], k_sem, 0, sibling)
    last.start()
    last.wait_send()
    remote(final.at[1 - core], final.at[1 - core], k_sem, 0, sibling).wait_recv()
    at = (y % 2) * 4 + core * 2
    out_ref[0] = final[0, pl.ds(at, 2), :]
    out_ref[1] = final[1, pl.ds(at, 2), :]


def sum_coefficients(coef):
    vmem = pl.BlockSpec(memory_space=pltpu.VMEM)
    sems = lambda count: pltpu.SemaphoreType.DMA((2, count))
    return pl.pallas_call(
        sum_kernel,
        in_specs=[vmem],
        out_specs=vmem,
        out_shape=jax.ShapeDtypeStruct((2, 2, 128), f32),
        scratch_shapes=[
            pltpu.VMEM((BLOCK, 128), f32),
            pltpu.VMEM((NZ, 32, 128), f32),
            pltpu.VMEM((NZ - 1, 32, 128), f32),
            pltpu.VMEM((4, 8, 128), f32),
            pltpu.VMEM((NY - 1, 8, 128), f32),
            pltpu.VMEM((2, 8, 128), f32),
            sems(1),
            sems(NZ - 1),
            sems(NY - 1),
            sems(1),
        ],
        compiler_params=pltpu.CompilerParams(collective_id=1, has_side_effects=True),
        name="coefficient_sum",
    )(coef)


def local(points, factor, targets, pivot_slots, pivot_counts):
    slots = jnp.broadcast_to(pivot_slots.reshape(2 * MAXP, 1), (2 * MAXP, 128))
    g = gather_pivots(slots, pivot_counts, points, factor)
    xs = [points]
    for d in range(1, NX):
        xs.append(lax.ppermute(points, "cols", [((i + d) % NX, i) for i in range(NX)]))
    inv, cross, sq = factor_pivots(g)
    new, res, coef = solve_rows(xs, factor, targets, g, inv, cross, sq)
    return new, res, sum_coefficients(coef)


def solution(mesh):
    in_specs = (P("rows", "cols"), P("rows", None), P("rows", "cols"), P(None, "rows"), P())
    out_specs = (P(None, "rows", "cols"), P(None, "rows"), P(None, "rows", "cols"))
    return jax.shard_map(local, mesh=mesh, in_specs=in_specs, out_specs=out_specs, check_vma=False)
```

```python
import functools
import jax
import jax.numpy as jnp
from jax import lax
from jax.experimental import pallas as pl
from jax.experimental.pallas import tpu as pltpu
from jax.sharding import PartitionSpec as P

F = 1024
BLOCK = 256
MAXP = 8
NX = 4
FQ = 256
KQ = 384
W = FQ + KQ
ROWS = 1024
TILE = 256
HI = lax.Precision.HIGHEST
f32 = jnp.float32
bf16 = jnp.bfloat16


def mm_nt(a, b, precision=None):
    return lax.dot_general(
        a, b, (((1,), (1,)), ((), ())), precision=precision, preferred_element_type=f32
    )


def mm_nn(a, b, precision=None):
    return lax.dot_general(
        a, b, (((1,), (0,)), ((), ())), precision=precision, preferred_element_type=f32
    )


def mm_tn(a, b):
    return lax.dot_general(a, b, (((0,), (0,)), ((), ())), preferred_element_type=f32)


def split2(a):
    high = a.astype(bf16)
    return high, (a - high.astype(f32)).astype(bf16)


def chol_inv_128(a):
    n = 16
    sub = lax.broadcasted_iota(jnp.int32, (8, 128), 0)
    lane = lax.broadcasted_iota(jnp.int32, (8, 128), 1)
    A = [a[8 * r : 8 * r + 8, :] for r in range(n)]
    X = [jnp.where(lane == sub + 8 * r, 1.0, 0.0).astype(f32) for r in range(n)]
    out = []
    for k in range(n):
        panel = [
            [jnp.broadcast_to(A[r][:, 8 * k + m : 8 * k + m + 1], (8, 128)) for m in range(8)]
            if r >= k
            else None
            for r in range(n)
        ]
        pivots = jnp.ones((8, 128), f32)
        for j in range(8):
            row = lambda v: jnp.broadcast_to(v[j : j + 1, :], (8, 128))
            row_a, row_x = row(A[k]), row(X[k])
            row_p = [row(panel[k][m]) if m >= j else None for m in range(8)]
            pivots = jnp.where(sub == j, row_p[j], pivots)
            inverse = 1.0 / row_p[j]
            for r in range(k, n):
                c = panel[r][j] * inverse
                if r == k:
                    if j == 7:
                        continue
                    c = jnp.where(sub > j, c, 0.0)
                A[r] = A[r] - c * row_a
                X[r] = X[r] - c * row_x
                for m in range(j + 1, 8):
                    panel[r][m] = panel[r][m] - c * row_p[m]
        out.append(X[k] * lax.rsqrt(pivots))
    return jnp.concatenate(out, axis=0)


def chol_inv_256(a):
    inv11 = chol_inv_128(a[:128, :128])
    low21 = mm_nt(a[128:, :128], inv11, HI)
    inv22 = chol_inv_128(a[128:, 128:] - mm_nt(low21, low21, HI))
    inv21 = -mm_nn(inv22, mm_nn(low21, inv11, HI), HI)
    zero = jnp.zeros((128, 128), f32)
    return jnp.concatenate(
        [jnp.concatenate([inv11, zero], axis=1), jnp.concatenate([inv21, inv22], axis=1)], axis=0
    )


def factor_kernel(g_ref, inv_ref, cross_ref, sq_ref):
    def gram(a, b):
        dots = sum(mm_nt(g_ref[c, a, :, :FQ], g_ref[c, b, :, :FQ]) for c in range(NX))
        basis = sum(mm_nt(g_ref[c, a, :, FQ:], g_ref[c, b, :, FQ:]) for c in range(NX))
        return dots, basis

    eye = lax.broadcasted_iota(jnp.int32, (256, 256), 0) == lax.broadcasted_iota(
        jnp.int32, (256, 256), 1
    )

    def norms(dots):
        diag = jnp.where(eye, dots, 0.0)
        return jnp.sum(diag, axis=1, keepdims=True), jnp.sum(diag, axis=0, keepdims=True)

    dots00, basis00 = gram(0, 0)
    dots10, basis10 = gram(1, 0)
    dots11, basis11 = gram(1, 1)
    col0, row0 = norms(dots00)
    col1, row1 = norms(dots11)
    sq_ref[:256] = jnp.broadcast_to(col0, (256, 128))
    sq_ref[256:] = jnp.broadcast_to(col1, (256, 128))
    a00 = jnp.exp(-(col0 + row0 - 2.0 * dots00) / F) - basis00
    a10 = jnp.exp(-(col1 + row0 - 2.0 * dots10) / F) - basis10
    a11 = jnp.exp(-(col1 + row1 - 2.0 * dots11) / F) - basis11
    inv0 = chol_inv_256(a00)
    narrow10 = mm_nt(a10, inv0, HI).astype(bf16)
    inv1 = chol_inv_256(a11 - mm_nt(narrow10, narrow10))
    cross_ref[...] = narrow10
    inv_ref[0, 0], inv_ref[0, 1] = split2(inv0)
    inv_ref[1, 0], inv_ref[1, 1] = split2(inv1)


def factor_pivots(g):
    return pl.pallas_call(
        factor_kernel,
        out_shape=(
            jax.ShapeDtypeStruct((2, 2, BLOCK, BLOCK), bf16),
            jax.ShapeDtypeStruct((BLOCK, BLOCK), bf16),
            jax.ShapeDtypeStruct((2 * BLOCK, 128), f32),
        ),
        compiler_params=pltpu.CompilerParams(vmem_limit_bytes=40 * 2**20),
        cost_estimate=pl.CostEstimate(
            flops=60_000_000_000, bytes_accessed=4_000_000, transcendentals=0
        ),
        name="pivot_factor",
    )(g)


def fold(v):
    total = v[:, :128]
    for i in range(1, v.shape[1] // 128):
        total = total + v[:, 128 * i : 128 * i + 128]
    return total


def rows_kernel(
    x0_ref, x1_ref, x2_ref, x3_ref, f_ref, t_ref, g_ref, inv_ref, cross_ref, sq_ref,
    new_ref, res_ref, coef_ref, all_ref,
):
    place = lax.axis_index("cols")
    dots = jnp.zeros((2 * BLOCK, TILE), f32)
    basis = jnp.zeros((2 * BLOCK, TILE), f32)
    squares = jnp.zeros((TILE, 128), f32)
    factor_squares = jnp.zeros((TILE, 128), f32)
    for c, x_ref in enumerate((x0_ref, x1_ref, x2_ref, x3_ref)):
        x = x_ref[...]
        fac = f_ref[:, KQ * c : KQ * c + KQ]
        dots = dots + mm_nt(g_ref[(place + c) % NX, :, :, :FQ].reshape(2 * BLOCK, FQ), x)
        basis = basis + mm_nt(g_ref[c, :, :, FQ:].reshape(2 * BLOCK, KQ), fac)
        squares = squares + fold(jnp.square(x.astype(f32)))
        factor_squares = factor_squares + fold(jnp.square(fac.astype(f32)))

    def across(v):
        return jnp.sum(jnp.transpose(v), axis=0, keepdims=True)

    columns = jnp.exp(-(sq_ref[:, 0:1] + across(squares) - 2.0 * dots) / F) - basis

    def solve(b, cols):
        high, low = split2(cols)
        return (
            mm_nn(inv_ref[b, 0], high) + mm_nn(inv_ref[b, 1], high) + mm_nn(inv_ref[b, 0], low)
        )

    @pl.when(pl.program_id(0) == 0)
    def _():
        coef_ref[...] = jnp.zeros_like(coef_ref)

    res = 1.0 - across(factor_squares)
    cols = columns[:BLOCK]
    for b in range(2):
        fresh = solve(b, cols)
        narrow = fresh.astype(bf16)
        if b == 0:
            cols = columns[BLOCK:] - mm_nn(cross_ref[...], narrow)
        all_ref[...] = fresh
        new_ref[b] = all_ref[pl.ds(pl.multiple_of(place * 64, 64), 64), :]
        res = res - jnp.sum(jnp.square(fresh), axis=0, keepdims=True)
        res_ref[b : b + 1, :] = res
        coef_ref[b] += mm_nn(narrow, t_ref[...])


def solve_rows(xs, factor, targets, g, inv, cross, sq):
    whole = lambda shape: pl.BlockSpec(shape, lambda i: (0,) * len(shape))
    return pl.pallas_call(
        rows_kernel,
        grid=(ROWS // TILE,),
        in_specs=[
            *[pl.BlockSpec((TILE, FQ), lambda i: (i, 0))] * NX,
            pl.BlockSpec((TILE, NX * KQ), lambda i: (i, 0)),
            pl.BlockSpec((TILE, 128), lambda i: (i, 0)),
            whole((NX, 2, BLOCK, W)),
            whole((2, 2, BLOCK, BLOCK)),
            whole((BLOCK, BLOCK)),
            whole((2 * BLOCK, 128)),
        ],
        out_specs=[
            pl.BlockSpec((2, 64, TILE), lambda i: (0, 0, i)),
            pl.BlockSpec((2, TILE), lambda i: (0, i)),
            whole((2, BLOCK, 128)),
        ],
        out_shape=(
            jax.ShapeDtypeStruct((2, 64, ROWS), f32),
            jax.ShapeDtypeStruct((2, ROWS), f32),
            jax.ShapeDtypeStruct((2, BLOCK, 128), f32),
        ),
        scratch_shapes=[pltpu.VMEM((BLOCK, TILE), f32)],
        compiler_params=pltpu.CompilerParams(vmem_limit_bytes=40 * 2**20),
        name="row_solve",
    )(*xs, factor, targets, g, inv, cross, sq)

NZ = 8
NY = 8
CORES = 2
PARTS = 4
MESH = pl.DeviceIdType.MESH


def spot():
    index = lax.axis_index("rows")
    return index // (NY * CORES), (index // CORES) % NY, index % CORES


def row_id(z, y, core):
    return {"rows": (z * NY + y) * CORES + core}


def enter(devices):
    barrier = pltpu.get_barrier_semaphore()
    for device in devices:
        pl.semaphore_signal(barrier, inc=1, device_id=device, device_id_type=MESH)
    return lambda: pl.semaphore_wait(barrier, len(devices))


def remote(src, dst, sems, index, device):
    return pltpu.make_async_remote_copy(
        src_ref=src,
        dst_ref=dst,
        send_sem=sems.at[0, index],
        recv_sem=sems.at[1, index],
        device_id=device,
        device_id_type=MESH,
    )


def gather_kernel(
    slots_ref, counts_ref, points_ref, factor_ref, g_ref, x1_ref, x2_ref, x3_ref,
    mine_points, quarter, own, other, buf_a, buf_b, load_sem,
    core_sem, ya_sem, zb_sem, za_sem, yb_sem, x_sem, k_sem, p_sem,
):
    z, y, core = spot()
    x = lax.axis_index("cols")
    sibling = row_id(z, y, 1 - core)
    y_peers = [row_id(z, (y + d) % NY, core) for d in range(1, NY)]
    z_peers = [row_id((z + d) % NZ, y, core) for d in range(1, NZ)]
    right, left = {"cols": (x + 1) % NX}, {"cols": (x + NX - 1) % NX}
    loads = [
        pltpu.make_async_copy(
            factor_ref.at[:, pl.ds(pl.multiple_of(x * KQ, 128), KQ)], quarter, load_sem.at[0]
        ),
        pltpu.make_async_copy(points_ref, mine_points, load_sem.at[1]),
    ]
    for load in loads:
        load.start()
    wait_entered = enter([sibling] + y_peers + z_peers + [right, left])

    diagonal = lax.broadcasted_iota(jnp.int32, (MAXP, MAXP), 0) == lax.broadcasted_iota(
        jnp.int32, (MAXP, MAXP), 1
    )
    slots = [
        jnp.sum(
            jnp.where(diagonal, slots_ref[b : b + 1, :].astype(f32), 0.0), axis=1, keepdims=True
        ).astype(jnp.int32)
        for b in range(2)
    ]
    point = lax.broadcasted_iota(jnp.int32, (MAXP, ROWS), 1)
    chosen = jnp.concatenate([(point == slot).astype(f32) for slot in slots], axis=0).astype(bf16)
    for load in loads:
        load.wait()
    own[:, :FQ] = mm_nn(chosen, mine_points[...]).astype(bf16)
    own[:, FQ:] = mm_nn(chosen, quarter[...]).astype(bf16)
    wait_entered()

    swap = remote(own, other, core_sem, 0, sibling)
    swap.start()
    far_half = ROWS // 2
    low, high = pl.ds(0, far_half), pl.ds(far_half, far_half)
    points_left = remote(points_ref, x1_ref, p_sem, 0, left)
    points_right = remote(points_ref, x3_ref, p_sem, 1, right)
    far_left = remote(x1_ref.at[low], x2_ref.at[low], p_sem, 2, left)
    far_right = remote(x3_ref.at[high], x2_ref.at[high], p_sem, 3, right)
    points_left.start()
    points_right.start()
    swap.wait()
    mine, theirs = own[...].astype(f32), other[...].astype(f32)
    first = core == 0
    pair = jnp.concatenate(
        [
            jnp.where(first, mine[:MAXP], theirs[MAXP:]),
            jnp.where(first, theirs[:MAXP], mine[MAXP:]),
        ],
        axis=0,
    ).astype(bf16)
    buf_a[z, y] = pair[:, FQ:]
    buf_b[y, z] = pair[:, :FQ]
    along_y = [
        remote(buf_a.at[z, y], buf_a.at[z, y], ya_sem, d, y_peers[d]) for d in range(NY - 1)
    ]
    along_z = [
        remote(buf_b.at[y, z], buf_b.at[y, z], zb_sem, d, z_peers[d]) for d in range(NZ - 1)
    ]
    for one, two in zip(along_y, along_z):
        one.start()
        two.start()

    counts = jnp.where(first, counts_ref[0:1, :], counts_ref[1:2, :]).astype(f32)
    counts = jnp.broadcast_to(counts, (8, 128)).astype(bf16)
    before = lax.broadcasted_iota(jnp.int32, (128, 128), 0) < lax.broadcasted_iota(
        jnp.int32, (128, 128), 1
    )
    offsets = mm_nn(counts, before.astype(bf16)).astype(bf16)
    owner_row = lax.broadcasted_iota(jnp.int32, (128, 1024), 0)
    column = lax.broadcasted_iota(jnp.int32, (128, 1024), 1)
    slot = (lax.broadcasted_iota(jnp.int32, (8, 1024), 1) % MAXP).astype(f32)
    pivot_row = lax.broadcasted_iota(jnp.int32, (BLOCK, 1024), 0)

    def places(owner_of):
        spread = (owner_row == owner_of(column // MAXP)).astype(bf16)
        start, count = mm_nn(offsets, spread), mm_nn(counts, spread)
        target = jnp.where(slot < count, start + slot, -1.0)
        return (pivot_row.astype(f32) == target[0:1, :]).astype(bf16)

    def swapped(position):
        return ((position // CORES) % NZ * NY + position // (CORES * NZ)) * CORES + position % CORES

    compact_a = places(lambda position: position)
    compact_b = places(swapped)

    for d in range(NY - 1):
        source = (y + NY - 1 - d) % NY
        remote(buf_a.at[z, source], buf_a.at[z, source], ya_sem, d, y_peers[d]).wait_recv()
    for d in range(NZ - 1):
        source = (z + NZ - 1 - d) % NZ
        remote(buf_b.at[y, source], buf_b.at[y, source], zb_sem, d, z_peers[d]).wait_recv()

    def ring(buf, sems, me, count, up, down):
        last = count // 2 - 1
        size = buf.shape[1] // PARTS

        def go_up(step, part, origin):
            piece = buf.at[origin % count, pl.ds(part * size, size)]
            return remote(piece, piece, sems, step * PARTS + part, up)

        def go_down(step, part, origin):
            piece = buf.at[origin % count, pl.ds(part * size, size)]
            return remote(piece, piece, sems, (last + 1 + step) * PARTS + part, down)

        goes_up = lambda step, part: step < last or part < PARTS // 2
        goes_down = lambda step, part: step < last or part >= PARTS // 2

        def send(step, part):
            if goes_up(step, part):
                go_up(step, part, me + count - step).start()
            if goes_down(step, part):
                go_down(step, part, me + step).start()

        def receive(step, part):
            if goes_up(step, part):
                go_up(step, part, me + count - 1 - step).wait_recv()
            if goes_down(step, part):
                go_down(step, part, me + 1 + step).wait_recv()

        def finish():
            for step in range(last + 1):
                for part in range(PARTS):
                    if goes_up(step, part):
                        go_up(step, part, me + count - step).wait_send()
                    if goes_down(step, part):
                        go_down(step, part, me + step).wait_send()

        return send, receive, finish

    rings = [
        ring(buf_a, za_sem, z, NZ, z_peers[0], z_peers[NZ - 2]),
        ring(buf_b, yb_sem, y, NY, y_peers[0], y_peers[NY - 2]),
    ]
    for part in range(PARTS):
        for send, receive, finish in rings:
            send(0, part)
    for step in range(NZ // 2):
        for part in range(PARTS):
            for send, receive, finish in rings:
                receive(step, part)
                if step + 1 < NZ // 2:
                    send(step + 1, part)
        if step == 1:
            points_left.wait_recv()
            far_left.start()
            points_right.wait_recv()
            far_right.start()

    g_ref[x, core, :, FQ:] = mm_nn(compact_a, buf_a[...].reshape(1024, KQ)).astype(bf16)
    g_ref[x, core, :, :FQ] = mm_nn(compact_b, buf_b[...].reshape(1024, FQ)).astype(bf16)

    half = BLOCK // 2
    x_left, x_right, x_far = (x + NX - 1) % NX, (x + 1) % NX, (x + 2) % NX

    def part(origin, at):
        return g_ref.at[origin, core, pl.ds(at * half, half), :]

    def to_right(origin, at, index):
        return remote(part(origin, at), part(origin, at), x_sem, index, right)

    def to_left(origin, at, index):
        return remote(part(origin, at), part(origin, at), x_sem, 3 + index, left)

    def to_sibling(origin):
        return remote(g_ref.at[origin, core], g_ref.at[origin, core], k_sem, origin, sibling)

    sends = [to_right(x, 0, 0), to_left(x, 1, 0), to_right(x, 1, 1), to_left(x, 0, 1), to_sibling(x)]
    for copy in sends:
        copy.start()
    to_right(x_left, 0, 0).wait_recv()
    sends.append(to_right(x_left, 0, 2))
    sends[-1].start()
    to_left(x_right, 1, 0).wait_recv()
    sends.append(to_left(x_right, 1, 2))
    sends[-1].start()
    to_right(x_left, 1, 1).wait_recv()
    sends.append(to_sibling(x_left))
    sends[-1].start()
    to_left(x_right, 0, 1).wait_recv()
    sends.append(to_sibling(x_right))
    sends[-1].start()
    to_right(x_far, 0, 2).wait_recv()
    to_left(x_far, 1, 2).wait_recv()
    sends.append(to_sibling(x_far))
    sends[-1].start()
    for origin in range(NX):
        arrived = g_ref.at[origin, 1 - core]
        remote(arrived, arrived, k_sem, origin, sibling).wait_recv()
    for copy in along_y + along_z + sends:
        copy.wait_send()
    for send, receive, finish in rings:
        finish()
    points_left.wait_send()
    points_right.wait_send()
    far_left.wait()
    far_right.wait()


def gather_pivots(slots, counts, points, factor):
    vmem = pl.BlockSpec(memory_space=pltpu.VMEM)
    hbm = pl.BlockSpec(memory_space=pltpu.HBM)
    sems = lambda count: pltpu.SemaphoreType.DMA((2, count))
    shape = jax.ShapeDtypeStruct((ROWS, FQ), bf16)
    return pl.pallas_call(
        gather_kernel,
        in_specs=[vmem, vmem, hbm, hbm],
        out_specs=[vmem, hbm, hbm, hbm],
        out_shape=(jax.ShapeDtypeStruct((NX, 2, BLOCK, W), bf16), shape, shape, shape),
        scratch_shapes=[
            pltpu.VMEM((ROWS, FQ), bf16),
            pltpu.VMEM((ROWS, KQ), bf16),
            pltpu.VMEM((2 * MAXP, W), bf16),
            pltpu.VMEM((2 * MAXP, W), bf16),
            pltpu.VMEM((NZ, NY, 2 * MAXP, KQ), bf16),
            pltpu.VMEM((NY, NZ, 2 * MAXP, FQ), bf16),
            pltpu.SemaphoreType.DMA((2,)),
            sems(1),
            sems(NY - 1),
            sems(NZ - 1),
            sems(NZ * PARTS),
            sems(NY * PARTS),
            sems(6),
            sems(NX),
            sems(4),
        ],
        compiler_params=pltpu.CompilerParams(
            collective_id=0, has_side_effects=True, vmem_limit_bytes=60 * 2**20
        ),
        name="pivot_gather",
    )(slots, counts, points, factor)


def sum_kernel(coef_ref, out_ref, got, total, got_z, piece, got_y, final, core_sem, z_sem, y_sem):
    z, y, core = spot()
    sibling = row_id(z, y, 1 - core)
    z_peers = [row_id((z + d) % NZ, y, core) for d in range(1, NZ)]
    y_same = [row_id(z, (y + d) % NY, core) for d in range(1, NY)]
    y_other = [row_id(z, (y + d) % NY, 1 - core) for d in range(NY)]
    enter(z_peers + y_same + y_other)()

    swap = remote(coef_ref.at[1 - core], got, core_sem, 0, sibling)
    swap.start()
    swap.wait()
    total[...] = (coef_ref[core] + got[...]).reshape(NZ, 32, 128)
    over_z = [
        remote(total.at[(z + d + 1) % NZ], got_z.at[d], z_sem, d, z_peers[d])
        for d in range(NZ - 1)
    ]
    for copy in over_z:
        copy.start()
    for copy in over_z:
        copy.wait()
    mine = total[z]
    for d in range(NZ - 1):
        mine = mine + got_z[d]
    piece[...] = mine.reshape(4, 8, 128)
    over_y = []
    for d in range(NY):
        tile = piece.at[(y + d) % NY // 2]
        if d:
            over_y.append(remote(tile, got_y.at[core, d], y_sem, d, y_same[d - 1]))
        over_y.append(remote(tile, got_y.at[core, d], y_sem, NY + d, y_other[d]))
    for copy in over_y:
        copy.start()
    got_y[core, 0] = piece[y // 2]
    for d in range(NY):
        if d:
            remote(piece.at[0], got_y.at[core, d], y_sem, d, y_same[d - 1]).wait_recv()
        remote(piece.at[0], got_y.at[1 - core, d], y_sem, NY + d, y_other[d]).wait_recv()
    for b in range(2):
        mine = got_y[b, 0]
        for d in range(1, NY):
            mine = mine + got_y[b, d]
        final[b] = mine
    at = (y % 2) * 4 + core * 2
    out_ref[0] = final[0, pl.ds(at, 2), :]
    out_ref[1] = final[1, pl.ds(at, 2), :]
    for copy in over_y:
        copy.wait_send()


def sum_coefficients(coef):
    vmem = pl.BlockSpec(memory_space=pltpu.VMEM)
    sems = lambda count: pltpu.SemaphoreType.DMA((2, count))
    return pl.pallas_call(
        sum_kernel,
        in_specs=[vmem],
        out_specs=vmem,
        out_shape=jax.ShapeDtypeStruct((2, 2, 128), f32),
        scratch_shapes=[
            pltpu.VMEM((BLOCK, 128), f32),
            pltpu.VMEM((NZ, 32, 128), f32),
            pltpu.VMEM((NZ - 1, 32, 128), f32),
            pltpu.VMEM((4, 8, 128), f32),
            pltpu.VMEM((2, NY, 8, 128), f32),
            pltpu.VMEM((2, 8, 128), f32),
            sems(1),
            sems(NZ - 1),
            sems(2 * NY),
        ],
        compiler_params=pltpu.CompilerParams(collective_id=1, has_side_effects=True),
        name="coefficient_sum",
    )(coef)


def local(points, factor, targets, pivot_slots, pivot_counts):
    g, *others = gather_pivots(pivot_slots, pivot_counts, points, factor)
    inv, cross, sq = factor_pivots(g)
    new, res, coef = solve_rows([points, *others], factor, targets, g, inv, cross, sq)
    return jnp.swapaxes(new, 1, 2), res, sum_coefficients(coef)


def solution(mesh):
    in_specs = (P("rows", "cols"), P("rows", None), P("rows", "cols"), P(None, "rows"), P())
    out_specs = (P(None, "rows", "cols"), P(None, "rows"), P(None, "rows", "cols"))
    return jax.shard_map(local, mesh=mesh, in_specs=in_specs, out_specs=out_specs, check_vma=False)
```

```python
import functools
import jax
import jax.numpy as jnp
from jax import lax
from jax.experimental import pallas as pl
from jax.experimental.pallas import tpu as pltpu
from jax.sharding import PartitionSpec as P

F = 1024
BLOCK = 256
MAXP = 8
NX = 4
FQ = 256
KQ = 384
W = FQ + KQ
ROWS = 1024
TILE = 256
HI = lax.Precision.HIGHEST
f32 = jnp.float32
bf16 = jnp.bfloat16


def mm_nt(a, b, precision=None):
    return lax.dot_general(
        a, b, (((1,), (1,)), ((), ())), precision=precision, preferred_element_type=f32
    )


def mm_nn(a, b, precision=None):
    return lax.dot_general(
        a, b, (((1,), (0,)), ((), ())), precision=precision, preferred_element_type=f32
    )


def mm_tn(a, b):
    return lax.dot_general(a, b, (((0,), (0,)), ((), ())), preferred_element_type=f32)


def split2(a):
    high = a.astype(bf16)
    return high, (a - high.astype(f32)).astype(bf16)


def nothing():
    pass


def chol_inv_128(a, beside=()):
    n = 16
    beside = list(beside)
    sub = lax.broadcasted_iota(jnp.int32, (8, 128), 0)
    lane = lax.broadcasted_iota(jnp.int32, (8, 128), 1)
    A = [a[8 * r : 8 * r + 8, :] for r in range(n)]
    X = [jnp.where(lane == sub + 8 * r, 1.0, 0.0).astype(f32) for r in range(n)]
    row = lambda v, j: jnp.broadcast_to(v[j : j + 1, :], (8, 128))
    out = []
    for k in range(n):
        columns = lambda v: [
            jnp.broadcast_to(v[:, 8 * k + m : 8 * k + m + 1], (8, 128)) for m in range(8)
        ]
        panel, own_a, own_x = columns(A[k]), A[k], X[k]
        pivots = jnp.ones((8, 128), f32)
        steps = []
        for j in range(8):
            row_p = [row(panel[m], j) if m >= j else None for m in range(8)]
            inverse = 1.0 / row_p[j]
            below = jnp.where(sub > j, panel[j], 0.0)
            for m in range(j + 1, 8):
                panel[m] = panel[m] - (below * row_p[m]) * inverse
            row_a, row_x = row(own_a, j), row(own_x, j)
            steps.append((row_a, row_x, row_p, inverse))
            pivots = jnp.where(sub == j, row_p[j], pivots)
            c = below * inverse
            own_a = own_a - c * row_a
            own_x = own_x - c * row_x
        out.append(own_x * lax.rsqrt(pivots))
        for r in range(k + 1, n):
            part = columns(A[r])
            for j, (row_a, row_x, row_p, inverse) in enumerate(steps):
                c = part[j] * inverse
                A[r] = A[r] - c * row_a
                X[r] = X[r] - c * row_x
                for m in range(j + 1, 8):
                    part[m] = part[m] - c * row_p[m]
        due = (len(beside) + n - 2 - k) // (n - 1 - k) if k < n - 1 else len(beside)
        for work in beside[:due]:
            work()
        beside = beside[due:]
    return jnp.concatenate(out, axis=0)


def chol_inv_256(a, beside=((), ())):
    inv11 = chol_inv_128(a[:128, :128], beside[0])
    low21 = mm_nt(a[128:, :128], inv11, HI)
    inv22 = chol_inv_128(a[128:, 128:] - mm_nt(low21, low21, HI), beside[1])
    inv21 = -mm_nn(inv22, mm_nn(low21, inv11, HI), HI)
    zero = jnp.zeros((128, 128), f32)
    return jnp.concatenate(
        [jnp.concatenate([inv11, zero], axis=1), jnp.concatenate([inv21, inv22], axis=1)], axis=0
    )


def fold(v):
    total = v[:, :128]
    for i in range(1, v.shape[1] // 128):
        total = total + v[:, 128 * i : 128 * i + 128]
    return total


def across(v):
    return jnp.sum(jnp.transpose(v), axis=0, keepdims=True)


def solve_kernel(
    g_hbm, x_hbm, f_hbm, t_hbm, new_ref, res_ref, coef_ref,
    g_ref, x_ref, f_ref, t_ref, columns, solved, narrow, squares, block10, block11, sems,
):
    place = lax.axis_index("cols")
    loads = [
        pltpu.make_async_copy(g_hbm.at[0], g_ref.at[0], sems.at[0]),
        pltpu.make_async_copy(g_hbm.at[1], g_ref.at[1], sems.at[1]),
        pltpu.make_async_copy(x_hbm, x_ref, sems.at[2]),
        pltpu.make_async_copy(f_hbm, f_ref, sems.at[3]),
        pltpu.make_async_copy(t_hbm, t_ref, sems.at[4]),
    ]
    for load in loads:
        load.start()
    eye = lax.broadcasted_iota(jnp.int32, (BLOCK, BLOCK), 0) == lax.broadcasted_iota(
        jnp.int32, (BLOCK, BLOCK), 1
    )

    def gram(a, b):
        dots = mm_nt(g_ref[a, :, :F], g_ref[b, :, :F])
        return dots, mm_nt(g_ref[a, :, F:], g_ref[b, :, F:])

    def kernel_matrix(col, row, dots, basis):
        return jnp.exp(-(col + row - 2.0 * dots) / F) - basis

    loads[0].wait()
    dots00, basis00 = gram(0, 0)
    diag = jnp.where(eye, dots00, 0.0)
    col0, row0 = jnp.sum(diag, axis=1, keepdims=True), jnp.sum(diag, axis=0, keepdims=True)
    a00 = kernel_matrix(col0, row0, dots00, basis00)

    cols = [col0, None]

    def tile(t):
        return pl.ds(t * TILE, TILE)

    def norms(t):
        def work():
            squares[0, :, tile(t)] = across(fold(jnp.square(x_ref[tile(t), :].astype(f32))))
            res_ref[0:1, tile(t)] = 1.0 - across(fold(jnp.square(f_ref[tile(t), :].astype(f32))))
        return work

    def fill(b, t):
        def work():
            dots = mm_nt(g_ref[b, :, :F], x_ref[tile(t), :])
            basis = mm_nt(g_ref[b, :, F:], f_ref[tile(t), :])
            columns[b, :, tile(t)] = kernel_matrix(cols[b], squares[0, :, tile(t)], dots, basis)
        return work

    def solve(b, inverse, t):
        high, low = split2(columns[b, :, tile(t)])
        fresh = mm_nn(inverse[0], high) + mm_nn(inverse[1], high) + mm_nn(inverse[0], low)
        solved[:, tile(t)] = fresh
        narrow[:, tile(t)] = fresh.astype(bf16)
        before = res_ref[0:1, tile(t)]
        res_ref[b : b + 1, tile(t)] = before - jnp.sum(jnp.square(fresh), axis=0, keepdims=True)

    tiles = range(ROWS // TILE)

    def later():
        for load in loads[1:]:
            load.wait()
        dots, basis = gram(1, 1)
        diag = jnp.where(eye, dots, 0.0)
        cols[1] = jnp.sum(diag, axis=1, keepdims=True)
        row1 = jnp.sum(diag, axis=0, keepdims=True)
        block11[...] = kernel_matrix(cols[1], row1, dots, basis)
        dots, basis = gram(1, 0)
        block10[...] = kernel_matrix(cols[1], row0, dots, basis)

    inv0 = chol_inv_256(
        a00,
        (
            [nothing] * 5 + [later] + [norms(t) for t in tiles],
            [fill(b, t) for b in range(2) for t in tiles],
        ),
    )
    split0 = split2(inv0)
    narrow10 = mm_nt(block10[...], inv0, HI).astype(bf16)
    a11 = block11[...] - mm_nt(narrow10, narrow10)

    def apply0(t):
        def work():
            solve(0, split0, t)
            columns[1, :, tile(t)] = columns[1, :, tile(t)] - mm_nn(narrow10, narrow[:, tile(t)])
        return work

    def emit(b):
        def work():
            new_ref[b] = solved[pl.ds(pl.multiple_of(place * 64, 64), 64), :]
        return work

    def coefficients(b):
        def work():
            coef_ref[b] = mm_nn(narrow[...], t_ref[...])
        return work

    inv1 = chol_inv_256(a11, ([apply0(t) for t in tiles], [emit(0), coefficients(0)]))
    split1 = split2(inv1)
    for t in tiles:
        solve(1, split1, t)
    coefficients(1)()
    emit(1)()


def solve_rows(g, x, factor, targets):
    any_ = pl.BlockSpec(memory_space=pl.ANY)
    vmem = pl.BlockSpec(memory_space=pltpu.VMEM)
    return pl.pallas_call(
        solve_kernel,
        in_specs=[any_] * 4,
        out_specs=[vmem] * 3,
        out_shape=(
            jax.ShapeDtypeStruct((2, 64, ROWS), f32),
            jax.ShapeDtypeStruct((2, ROWS), f32),
            jax.ShapeDtypeStruct((2, BLOCK, 128), f32),
        ),
        scratch_shapes=[
            pltpu.VMEM((2, BLOCK, NX * W), bf16),
            pltpu.VMEM((ROWS, F), bf16),
            pltpu.VMEM((ROWS, NX * KQ), bf16),
            pltpu.VMEM((ROWS, 128), bf16),
            pltpu.VMEM((2, BLOCK, ROWS), f32),
            pltpu.VMEM((BLOCK, ROWS), f32),
            pltpu.VMEM((BLOCK, ROWS), bf16),
            pltpu.VMEM((1, 1, ROWS), f32),
            pltpu.VMEM((BLOCK, BLOCK), f32),
            pltpu.VMEM((BLOCK, BLOCK), f32),
            pltpu.SemaphoreType.DMA((5,)),
        ],
        compiler_params=pltpu.CompilerParams(vmem_limit_bytes=60 * 2**20),
        name="pivot_solve",
    )(g, x, factor, targets)


NZ = 8
NY = 8
CORES = 2
PARTS = 2
MESH = pl.DeviceIdType.MESH


def spot():
    index = lax.axis_index("rows")
    return index // (NY * CORES), (index // CORES) % NY, index % CORES


def row_id(z, y, core):
    return {"rows": (z * NY + y) * CORES + core}


def enter(devices):
    barrier = pltpu.get_barrier_semaphore()
    for device in devices:
        pl.semaphore_signal(barrier, inc=1, device_id=device, device_id_type=MESH)
    return lambda: pl.semaphore_wait(barrier, len(devices))


def remote(src, dst, sems, index, device):
    return pltpu.make_async_remote_copy(
        src_ref=src,
        dst_ref=dst,
        send_sem=sems.at[0, index],
        recv_sem=sems.at[1, index],
        device_id=device,
        device_id_type=MESH,
    )


STREAMS = (
    (0, 128, False, lambda o: FQ * o),
    (FQ, 128, True, lambda o: F + KQ * o),
    (128, 128, False, lambda o: FQ * o + 128),
    (FQ + 128, 256, True, lambda o: F + KQ * o + 128),
)


def gather_kernel(slots_ref, counts_ref, points_ref, factor_ref, g_ref, x_ref, *scratch):
    mine_points, quarter, own, other, load_sem, core_sem, p_sem = scratch[:7]
    bufs, line_sems, ring_sems, x_sems, k_sems = [scratch[7 + 4 * i : 11 + 4 * i] for i in range(5)]
    z, y, core = spot()
    x = lax.axis_index("cols")
    sibling = row_id(z, y, 1 - core)
    y_peers = [row_id(z, (y + d) % NY, core) for d in range(1, NY)]
    z_peers = [row_id((z + d) % NZ, y, core) for d in range(1, NZ)]
    right, left = {"cols": (x + 1) % NX}, {"cols": (x + NX - 1) % NX}
    x_left, x_right, x_far = (x + NX - 1) % NX, (x + 1) % NX, (x + 2) % NX

    def lanes(start, width):
        return pl.ds(pl.multiple_of(start, 128), width)

    loads = [
        pltpu.make_async_copy(factor_ref.at[:, lanes(x * KQ, KQ)], quarter, load_sem.at[0]),
        pltpu.make_async_copy(points_ref, mine_points, load_sem.at[1]),
    ]
    keep = pltpu.make_async_copy(points_ref, x_ref.at[:, lanes(x * FQ, FQ)], load_sem.at[2])
    for load in loads:
        load.start()
    wait_entered = enter([sibling] + y_peers + z_peers + [right, left])

    diagonal = lax.broadcasted_iota(jnp.int32, (MAXP, MAXP), 0) == lax.broadcasted_iota(
        jnp.int32, (MAXP, MAXP), 1
    )
    slots = [
        jnp.sum(
            jnp.where(diagonal, slots_ref[b : b + 1, :].astype(f32), 0.0), axis=1, keepdims=True
        ).astype(jnp.int32)
        for b in range(2)
    ]
    point = lax.broadcasted_iota(jnp.int32, (MAXP, ROWS), 1)
    chosen = jnp.concatenate([(point == slot).astype(f32) for slot in slots], axis=0).astype(bf16)
    for load in loads:
        load.wait()
    own[:, :FQ] = mm_nn(chosen, mine_points[...]).astype(bf16)
    own[:, FQ:] = mm_nn(chosen, quarter[...]).astype(bf16)
    wait_entered()

    swap = remote(own, other, core_sem, 0, sibling)
    swap.start()
    half_rows = ROWS // 2

    def share(index, origin, start, count, device):
        part = x_ref.at[pl.ds(start, count), lanes(origin * FQ, FQ)]
        source = points_ref if index < 2 else part
        return remote(source, part, p_sem, index, device)

    share(0, x, 0, ROWS, left).start()
    share(1, x, 0, ROWS, right).start()
    keep.start()
    swap.wait()
    mine, theirs = own[...].astype(f32), other[...].astype(f32)
    first = core == 0
    pair = jnp.concatenate(
        [
            jnp.where(first, mine[:MAXP], theirs[MAXP:]),
            jnp.where(first, theirs[:MAXP], mine[MAXP:]),
        ],
        axis=0,
    ).astype(bf16)

    lines, rings = [], []
    for i, (start, width, y_first, _) in enumerate(STREAMS):
        here, there, peers = (z, y, y_peers) if y_first else (y, z, z_peers)
        bufs[i][here, there] = pair[:, start : start + width]
        part = bufs[i].at[here, there]
        lines.append([remote(part, part, line_sems[i], d, peers[d]) for d in range(NY - 1)])
    for d in (3, 2, 4, 1, 5, 0, 6):
        for line in lines:
            line[d].start()

    counts = jnp.where(first, counts_ref[0:1, :], counts_ref[1:2, :]).astype(f32)
    counts = jnp.broadcast_to(counts, (8, 128)).astype(bf16)
    before = lax.broadcasted_iota(jnp.int32, (128, 128), 0) < lax.broadcasted_iota(
        jnp.int32, (128, 128), 1
    )
    offsets = mm_nn(counts, before.astype(bf16)).astype(bf16)
    owner_row = lax.broadcasted_iota(jnp.int32, (128, 1024), 0)
    column = lax.broadcasted_iota(jnp.int32, (128, 1024), 1)
    slot = (lax.broadcasted_iota(jnp.int32, (8, 1024), 1) % MAXP).astype(f32)
    pivot_row = lax.broadcasted_iota(jnp.int32, (BLOCK, 1024), 0)

    def places(owner_of):
        spread = (owner_row == owner_of(column // MAXP)).astype(bf16)
        start, count = mm_nn(offsets, spread), mm_nn(counts, spread)
        target = jnp.where(slot < count, start + slot, -1.0)
        return (pivot_row.astype(f32) == target[0:1, :]).astype(bf16)

    def swapped(position):
        return ((position // CORES) % NZ * NY + position // (CORES * NZ)) * CORES + position % CORES

    compact = (places(swapped), places(lambda position: position))

    for i, (start, width, y_first, _) in enumerate(STREAMS):
        here, there, peers = (z, y, y_peers) if y_first else (y, z, z_peers)
        for d in range(NY - 1):
            part = bufs[i].at[here, (there + NY - 1 - d) % NY]
            remote(part, part, line_sems[i], d, peers[d]).wait_recv()

    def ring(buf, sems, me, count, up, down):
        last = count // 2 - 1
        size = buf.shape[1] // PARTS

        def go_up(step, part, origin):
            piece = buf.at[origin % count, pl.ds(part * size, size)]
            return remote(piece, piece, sems, step * PARTS + part, up)

        def go_down(step, part, origin):
            piece = buf.at[origin % count, pl.ds(part * size, size)]
            return remote(piece, piece, sems, (last + 1 + step) * PARTS + part, down)

        goes_up = lambda step, part: step < last or part < PARTS // 2
        goes_down = lambda step, part: step < last or part >= PARTS // 2

        def send(step, part):
            if goes_up(step, part):
                go_up(step, part, me + count - step).start()
            if goes_down(step, part):
                go_down(step, part, me + step).start()

        def receive(step, part):
            if goes_up(step, part):
                go_up(step, part, me + count - 1 - step).wait_recv()
            if goes_down(step, part):
                go_down(step, part, me + 1 + step).wait_recv()

        def finish():
            for step in range(last + 1):
                for part in range(PARTS):
                    if goes_up(step, part):
                        go_up(step, part, me + count - step).wait_send()
                    if goes_down(step, part):
                        go_down(step, part, me + step).wait_send()

        return send, receive, finish

    for i, (start, width, y_first, _) in enumerate(STREAMS):
        me, peers = (z, z_peers) if y_first else (y, y_peers)
        rings.append(ring(bufs[i], ring_sems[i], me, NZ, peers[0], peers[NZ - 2]))
    pairs = ((0, 1), (2, 3))

    def go(wave, step):
        for part in range(PARTS):
            for i in pairs[wave]:
                if step:
                    rings[i][1](step - 1, part)
                if step < NZ // 2:
                    rings[i][0](step, part)

    half = BLOCK // 2
    sends = []

    def part(i, origin, at, count=half):
        place = STREAMS[i][3](origin)
        return g_ref.at[core, pl.ds(at * half, count), lanes(place, STREAMS[i][1])]

    def to_right(i, origin, at, index):
        return remote(part(i, origin, at), part(i, origin, at), x_sems[i], index, right)

    def to_left(i, origin, at, index):
        return remote(part(i, origin, at), part(i, origin, at), x_sems[i], 3 + index, left)

    def to_sibling(i, origin, index):
        block = part(i, origin, 0, BLOCK)
        return remote(block, block, k_sems[i], index, sibling)

    def begin(copy):
        sends.append(copy)
        copy.start()

    def join(wave):
        for i in pairs[wave]:
            width, y_first = STREAMS[i][1:3]
            rows = bufs[i][...].reshape(1024, width)
            placed = mm_nn(compact[int(y_first)], rows).astype(bf16)
            g_ref[core, :, lanes(STREAMS[i][3](x), width)] = placed
        for i in pairs[wave]:
            begin(to_right(i, x, 0, 0))
            begin(to_left(i, x, 1, 0))
        for i in pairs[wave]:
            begin(to_right(i, x, 1, 1))
            begin(to_left(i, x, 0, 1))
            begin(to_sibling(i, x, 0))

    def forward(wave):
        for i in pairs[wave]:
            to_right(i, x_left, 0, 0).wait_recv()
            begin(to_right(i, x_left, 0, 2))
            to_left(i, x_right, 1, 0).wait_recv()
            begin(to_left(i, x_right, 1, 2))

    def collect(wave):
        for i in pairs[wave]:
            to_right(i, x_left, 1, 1).wait_recv()
            begin(to_sibling(i, x_left, 1))
            to_left(i, x_right, 0, 1).wait_recv()
            begin(to_sibling(i, x_right, 2))

    def close(wave):
        for i in pairs[wave]:
            to_right(i, x_far, 0, 2).wait_recv()
            to_left(i, x_far, 1, 2).wait_recv()
            begin(to_sibling(i, x_far, 3))

    go(0, 0)
    go(1, 0)
    go(0, 1)
    go(0, 2)
    go(1, 1)
    share(0, x_right, 0, ROWS, left).wait_recv()
    share(2, x_right, 0, half_rows, left).start()
    share(1, x_left, 0, ROWS, right).wait_recv()
    share(3, x_left, half_rows, half_rows, right).start()
    go(0, 3)
    go(1, 2)
    go(0, 4)
    join(0)
    go(1, 3)
    forward(0)
    go(1, 4)
    join(1)
    collect(0)
    close(0)
    forward(1)
    collect(1)
    close(1)
    for i in range(len(STREAMS)):
        for index, origin in enumerate((x, x_left, x_right, x_far)):
            block = g_ref.at[1 - core, :, lanes(STREAMS[i][3](origin), STREAMS[i][1])]
            remote(block, block, k_sems[i], index, sibling).wait_recv()
    share(2, x_far, 0, half_rows, left).wait_recv()
    share(3, x_far, half_rows, half_rows, right).wait_recv()
    share(0, x, 0, ROWS, left).wait_send()
    share(1, x, 0, ROWS, right).wait_send()
    share(2, x_right, 0, half_rows, left).wait_send()
    share(3, x_left, half_rows, half_rows, right).wait_send()
    keep.wait()
    for line in lines:
        for copy in line:
            copy.wait_send()
    for copy in sends:
        copy.wait_send()
    for send, receive, finish in rings:
        finish()


def gather_pivots(slots, counts, points, factor):
    vmem = pl.BlockSpec(memory_space=pltpu.VMEM)
    hbm = pl.BlockSpec(memory_space=pltpu.HBM)
    sems = lambda count: pltpu.SemaphoreType.DMA((2, count))
    each = len(STREAMS)
    return pl.pallas_call(
        gather_kernel,
        in_specs=[vmem, vmem, hbm, hbm],
        out_specs=[vmem, hbm],
        out_shape=(
            jax.ShapeDtypeStruct((2, BLOCK, NX * W), bf16),
            jax.ShapeDtypeStruct((ROWS, F), bf16),
        ),
        scratch_shapes=[
            pltpu.VMEM((ROWS, FQ), bf16),
            pltpu.VMEM((ROWS, KQ), bf16),
            pltpu.VMEM((2 * MAXP, W), bf16),
            pltpu.VMEM((2 * MAXP, W), bf16),
            pltpu.SemaphoreType.DMA((3,)),
            sems(1),
            sems(4),
            *[pltpu.VMEM((NZ, NY, 2 * MAXP, stream[1]), bf16) for stream in STREAMS],
            *[sems(NY - 1)] * each,
            *[sems(NZ * PARTS)] * each,
            *[sems(6)] * each,
            *[sems(NX)] * each,
        ],
        compiler_params=pltpu.CompilerParams(
            collective_id=0, has_side_effects=True, vmem_limit_bytes=60 * 2**20
        ),
        name="pivot_gather",
    )(slots, counts, points, factor)


def sum_kernel(coef_ref, out_ref, got, total, got_z, piece, got_y, final, core_sem, z_sem, y_sem):
    z, y, core = spot()
    sibling = row_id(z, y, 1 - core)
    z_peers = [row_id((z + d) % NZ, y, core) for d in range(1, NZ)]
    y_same = [row_id(z, (y + d) % NY, core) for d in range(1, NY)]
    y_other = [row_id(z, (y + d) % NY, 1 - core) for d in range(NY)]
    enter(z_peers + y_same + y_other)()

    swap = remote(coef_ref.at[1 - core], got, core_sem, 0, sibling)
    swap.start()
    swap.wait()
    total[...] = (coef_ref[core] + got[...]).reshape(NZ, 32, 128)
    over_z = [
        remote(total.at[(z + d + 1) % NZ], got_z.at[d], z_sem, d, z_peers[d])
        for d in range(NZ - 1)
    ]
    for copy in over_z:
        copy.start()
    for copy in over_z:
        copy.wait()
    mine = total[z]
    for d in range(NZ - 1):
        mine = mine + got_z[d]
    piece[...] = mine.reshape(4, 8, 128)
    over_y = []
    for d in range(NY):
        tile = piece.at[(y + d) % NY // 2]
        if d:
            over_y.append(remote(tile, got_y.at[core, d], y_sem, d, y_same[d - 1]))
        over_y.append(remote(tile, got_y.at[core, d], y_sem, NY + d, y_other[d]))
    for copy in over_y:
        copy.start()
    got_y[core, 0] = piece[y // 2]
    for d in range(NY):
        if d:
            remote(piece.at[0], got_y.at[core, d], y_sem, d, y_same[d - 1]).wait_recv()
        remote(piece.at[0], got_y.at[1 - core, d], y_sem, NY + d, y_other[d]).wait_recv()
    for b in range(2):
        mine = got_y[b, 0]
        for d in range(1, NY):
            mine = mine + got_y[b, d]
        final[b] = mine
    at = (y % 2) * 4 + core * 2
    out_ref[0] = final[0, pl.ds(at, 2), :]
    out_ref[1] = final[1, pl.ds(at, 2), :]
    for copy in over_y:
        copy.wait_send()


def sum_coefficients(coef):
    vmem = pl.BlockSpec(memory_space=pltpu.VMEM)
    sems = lambda count: pltpu.SemaphoreType.DMA((2, count))
    return pl.pallas_call(
        sum_kernel,
        in_specs=[vmem],
        out_specs=vmem,
        out_shape=jax.ShapeDtypeStruct((2, 2, 128), f32),
        scratch_shapes=[
            pltpu.VMEM((BLOCK, 128), f32),
            pltpu.VMEM((NZ, 32, 128), f32),
            pltpu.VMEM((NZ - 1, 32, 128), f32),
            pltpu.VMEM((4, 8, 128), f32),
            pltpu.VMEM((2, NY, 8, 128), f32),
            pltpu.VMEM((2, 8, 128), f32),
            sems(1),
            sems(NZ - 1),
            sems(2 * NY),
        ],
        compiler_params=pltpu.CompilerParams(collective_id=1, has_side_effects=True),
        name="coefficient_sum",
    )(coef)


def local(points, factor, targets, pivot_slots, pivot_counts):
    g, x = gather_pivots(pivot_slots, pivot_counts, points, factor)
    new, res, coef = solve_rows(g, x, factor, targets)
    return jnp.swapaxes(new, 1, 2), res, sum_coefficients(coef)


def solution(mesh):
    in_specs = (P("rows", "cols"), P("rows", None), P("rows", "cols"), P(None, "rows"), P())
    out_specs = (P(None, "rows", "cols"), P(None, "rows"), P(None, "rows", "cols"))
    return jax.shard_map(local, mesh=mesh, in_specs=in_specs, out_specs=out_specs, check_vma=False)
```

```python
import functools
import jax
import jax.numpy as jnp
from jax import lax
from jax.experimental import pallas as pl
from jax.experimental.pallas import tpu as pltpu
from jax.sharding import PartitionSpec as P

F = 1024
BLOCK = 256
MAXP = 8
NX = 4
FQ = 256
KQ = 384
W = FQ + KQ
ROWS = 1024
TILE = 256
HI = lax.Precision.HIGHEST
f32 = jnp.float32
bf16 = jnp.bfloat16


def mm_nt(a, b, precision=None):
    return lax.dot_general(
        a, b, (((1,), (1,)), ((), ())), precision=precision, preferred_element_type=f32
    )


def mm_nn(a, b, precision=None):
    return lax.dot_general(
        a, b, (((1,), (0,)), ((), ())), precision=precision, preferred_element_type=f32
    )


def mm_tn(a, b):
    return lax.dot_general(a, b, (((0,), (0,)), ((), ())), preferred_element_type=f32)


def split2(a):
    high = a.astype(bf16)
    return high, (a - high.astype(f32)).astype(bf16)


def nothing():
    pass


def chol_inv_128(a, beside=()):
    n = 16
    beside = list(beside)
    sub = lax.broadcasted_iota(jnp.int32, (8, 128), 0)
    lane = lax.broadcasted_iota(jnp.int32, (8, 128), 1)
    A = [a[8 * r : 8 * r + 8, :] for r in range(n)]
    X = [jnp.where(lane == sub + 8 * r, 1.0, 0.0).astype(f32) for r in range(n)]
    row = lambda v, j: jnp.broadcast_to(v[j : j + 1, :], (8, 128))
    out = []
    for k in range(n):
        columns = lambda v: [
            jnp.broadcast_to(v[:, 8 * k + m : 8 * k + m + 1], (8, 128)) for m in range(8)
        ]
        panel, own_a, own_x = columns(A[k]), A[k], X[k]
        pivots = jnp.ones((8, 128), f32)
        steps = []
        for j in range(8):
            row_p = [row(panel[m], j) if m >= j else None for m in range(8)]
            inverse = 1.0 / row_p[j]
            below = jnp.where(sub > j, panel[j], 0.0)
            for m in range(j + 1, 8):
                panel[m] = panel[m] - (below * row_p[m]) * inverse
            row_a, row_x = row(own_a, j), row(own_x, j)
            steps.append((row_a, row_x, row_p, inverse))
            pivots = jnp.where(sub == j, row_p[j], pivots)
            c = below * inverse
            own_a = own_a - c * row_a
            own_x = own_x - c * row_x
        out.append(own_x * lax.rsqrt(pivots))
        for r in range(k + 1, n):
            part = columns(A[r])
            for j, (row_a, row_x, row_p, inverse) in enumerate(steps):
                c = part[j] * inverse
                A[r] = A[r] - c * row_a
                X[r] = X[r] - c * row_x
                for m in range(j + 1, 8):
                    part[m] = part[m] - c * row_p[m]
        due = (len(beside) + n - 2 - k) // (n - 1 - k) if k < n - 1 else len(beside)
        for work in beside[:due]:
            work()
        beside = beside[due:]
    return jnp.concatenate(out, axis=0)


def chol_inv_256(a, beside=((), ())):
    inv11 = chol_inv_128(a[:128, :128], beside[0])
    low21 = mm_nt(a[128:, :128], inv11, HI)
    inv22 = chol_inv_128(a[128:, 128:] - mm_nt(low21, low21, HI), beside[1])
    inv21 = -mm_nn(inv22, mm_nn(low21, inv11, HI), HI)
    zero = jnp.zeros((128, 128), f32)
    return jnp.concatenate(
        [jnp.concatenate([inv11, zero], axis=1), jnp.concatenate([inv21, inv22], axis=1)], axis=0
    )


def lanes(start, width):
    return pl.ds(pl.multiple_of(start, 128), width)


def fold(v):
    total = v[:, :128]
    for i in range(1, v.shape[1] // 128):
        total = total + v[:, 128 * i : 128 * i + 128]
    return total


def across(v):
    return jnp.sum(jnp.transpose(v), axis=0, keepdims=True)


def solve_kernel(
    g_hbm, p_hbm, x_hbm, f_hbm, t_hbm, new_ref, res_ref, coef_ref,
    g_ref, x_ref, f_ref, t_ref, columns, solved, narrow, squares, block10, block11, sems,
):
    place = lax.axis_index("cols")
    loads = [
        pltpu.make_async_copy(g_hbm.at[0], g_ref.at[0], sems.at[0]),
        pltpu.make_async_copy(g_hbm.at[1], g_ref.at[1], sems.at[1]),
        pltpu.make_async_copy(f_hbm, f_ref, sems.at[2]),
        pltpu.make_async_copy(t_hbm, t_ref, sems.at[3]),
        pltpu.make_async_copy(p_hbm, x_ref.at[:, lanes(place * FQ, FQ)], sems.at[4]),
    ]
    for d in range(1, NX):
        part = lanes((place + d) % NX * FQ, FQ)
        loads.append(pltpu.make_async_copy(x_hbm.at[:, part], x_ref.at[:, part], sems.at[4 + d]))
    for load in loads:
        load.start()
    eye = lax.broadcasted_iota(jnp.int32, (BLOCK, BLOCK), 0) == lax.broadcasted_iota(
        jnp.int32, (BLOCK, BLOCK), 1
    )

    def gram(a, b):
        dots = mm_nt(g_ref[a, :, :F], g_ref[b, :, :F])
        return dots, mm_nt(g_ref[a, :, F:], g_ref[b, :, F:])

    def kernel_matrix(col, row, dots, basis):
        return jnp.exp(-(col + row - 2.0 * dots) / F) - basis

    loads[0].wait()
    dots00, basis00 = gram(0, 0)
    diag = jnp.where(eye, dots00, 0.0)
    col0, row0 = jnp.sum(diag, axis=1, keepdims=True), jnp.sum(diag, axis=0, keepdims=True)
    a00 = kernel_matrix(col0, row0, dots00, basis00)

    cols = [col0, None]

    def tile(t):
        return pl.ds(t * TILE, TILE)

    def norms(t):
        def work():
            squares[0, :, tile(t)] = across(fold(jnp.square(x_ref[tile(t), :].astype(f32))))
            res_ref[0:1, tile(t)] = 1.0 - across(fold(jnp.square(f_ref[tile(t), :].astype(f32))))
        return work

    def fill(b, t):
        def work():
            dots = mm_nt(g_ref[b, :, :F], x_ref[tile(t), :])
            basis = mm_nt(g_ref[b, :, F:], f_ref[tile(t), :])
            columns[b, :, tile(t)] = kernel_matrix(cols[b], squares[0, :, tile(t)], dots, basis)
        return work

    def solve(b, inverse, t):
        high, low = split2(columns[b, :, tile(t)])
        fresh = mm_nn(inverse[0], high) + mm_nn(inverse[1], high) + mm_nn(inverse[0], low)
        solved[:, tile(t)] = fresh
        narrow[:, tile(t)] = fresh.astype(bf16)
        before = res_ref[0:1, tile(t)]
        res_ref[b : b + 1, tile(t)] = before - jnp.sum(jnp.square(fresh), axis=0, keepdims=True)

    tiles = range(ROWS // TILE)

    def later():
        for load in loads[1:]:
            load.wait()
        dots, basis = gram(1, 1)
        diag = jnp.where(eye, dots, 0.0)
        cols[1] = jnp.sum(diag, axis=1, keepdims=True)
        row1 = jnp.sum(diag, axis=0, keepdims=True)
        block11[...] = kernel_matrix(cols[1], row1, dots, basis)
        dots, basis = gram(1, 0)
        block10[...] = kernel_matrix(cols[1], row0, dots, basis)

    inv0 = chol_inv_256(
        a00,
        (
            [nothing] * 5 + [later] + [norms(t) for t in tiles],
            [fill(b, t) for b in range(2) for t in tiles],
        ),
    )
    split0 = split2(inv0)
    narrow10 = mm_nt(block10[...], inv0, HI).astype(bf16)
    a11 = block11[...] - mm_nt(narrow10, narrow10)

    def apply0(t):
        def work():
            solve(0, split0, t)
            columns[1, :, tile(t)] = columns[1, :, tile(t)] - mm_nn(narrow10, narrow[:, tile(t)])
        return work

    def emit(b):
        def work():
            new_ref[b] = solved[pl.ds(pl.multiple_of(place * 64, 64), 64), :]
        return work

    def coefficients(b):
        def work():
            coef_ref[b] = mm_nn(narrow[...], t_ref[...])
        return work

    inv1 = chol_inv_256(a11, ([apply0(t) for t in tiles], [emit(0), coefficients(0)]))
    split1 = split2(inv1)
    for t in tiles:
        solve(1, split1, t)
    coefficients(1)()
    emit(1)()


def solve_rows(g, points, x, factor, targets):
    any_ = pl.BlockSpec(memory_space=pl.ANY)
    vmem = pl.BlockSpec(memory_space=pltpu.VMEM)
    return pl.pallas_call(
        solve_kernel,
        in_specs=[any_] * 5,
        out_specs=[vmem] * 3,
        out_shape=(
            jax.ShapeDtypeStruct((2, 64, ROWS), f32),
            jax.ShapeDtypeStruct((2, ROWS), f32),
            jax.ShapeDtypeStruct((2, BLOCK, 128), f32),
        ),
        scratch_shapes=[
            pltpu.VMEM((2, BLOCK, NX * W), bf16),
            pltpu.VMEM((ROWS, F), bf16),
            pltpu.VMEM((ROWS, NX * KQ), bf16),
            pltpu.VMEM((ROWS, 128), bf16),
            pltpu.VMEM((2, BLOCK, ROWS), f32),
            pltpu.VMEM((BLOCK, ROWS), f32),
            pltpu.VMEM((BLOCK, ROWS), bf16),
            pltpu.VMEM((1, 1, ROWS), f32),
            pltpu.VMEM((BLOCK, BLOCK), f32),
            pltpu.VMEM((BLOCK, BLOCK), f32),
            pltpu.SemaphoreType.DMA((8,)),
        ],
        compiler_params=pltpu.CompilerParams(vmem_limit_bytes=60 * 2**20),
        name="pivot_solve",
    )(g, points, x, factor, targets)


NZ = 8
NY = 8
CORES = 2
PARTS = 4
RECEIVED = (NZ - 1) * PARTS
MESH = pl.DeviceIdType.MESH


def spot():
    index = lax.axis_index("rows")
    return index // (NY * CORES), (index // CORES) % NY, index % CORES


def row_id(z, y, core):
    return {"rows": (z * NY + y) * CORES + core}


def enter(devices):
    barrier = pltpu.get_barrier_semaphore()
    for device in devices:
        pl.semaphore_signal(barrier, inc=1, device_id=device, device_id_type=MESH)
    return lambda: pl.semaphore_wait(barrier, len(devices))


def remote(src, dst, sems, index, device):
    return pltpu.make_async_remote_copy(
        src_ref=src,
        dst_ref=dst,
        send_sem=sems.at[0],
        recv_sem=sems.at[1 + index],
        device_id=device,
        device_id_type=MESH,
    )


STREAMS = (
    (0, FQ, False, lambda o: FQ * o),
    (FQ, KQ, True, lambda o: F + KQ * o),
)


def gather_kernel(slots_ref, counts_ref, points_ref, factor_ref, g_ref, x_ref, *scratch):
    mine_points, quarter, own, other, load_sem, core_sem = scratch[:6]
    p_sems = scratch[6:10]
    n = len(STREAMS)
    bufs, line_sems, ring_sems, x_sems, k_sems = [scratch[10 + n * i : 10 + n + n * i] for i in range(5)]
    z, y, core = spot()
    x = lax.axis_index("cols")
    sibling = row_id(z, y, 1 - core)
    y_peers = [row_id(z, (y + d) % NY, core) for d in range(1, NY)]
    z_peers = [row_id((z + d) % NZ, y, core) for d in range(1, NZ)]
    right, left = {"cols": (x + 1) % NX}, {"cols": (x + NX - 1) % NX}
    x_left, x_right, x_far = (x + NX - 1) % NX, (x + 1) % NX, (x + 2) % NX

    loads = [
        pltpu.make_async_copy(factor_ref.at[:, lanes(x * KQ, KQ)], quarter, load_sem.at[0]),
        pltpu.make_async_copy(points_ref, mine_points, load_sem.at[1]),
    ]
    for load in loads:
        load.start()
    wait_entered = enter([sibling] + y_peers + z_peers + [right, left])

    diagonal = lax.broadcasted_iota(jnp.int32, (MAXP, MAXP), 0) == lax.broadcasted_iota(
        jnp.int32, (MAXP, MAXP), 1
    )
    slots = [
        jnp.sum(
            jnp.where(diagonal, slots_ref[b : b + 1, :].astype(f32), 0.0), axis=1, keepdims=True
        ).astype(jnp.int32)
        for b in range(2)
    ]
    point = lax.broadcasted_iota(jnp.int32, (MAXP, ROWS), 1)
    chosen = jnp.concatenate([(point == slot).astype(f32) for slot in slots], axis=0).astype(bf16)
    for load in loads:
        load.wait()
    own[:, :FQ] = mm_nn(chosen, mine_points[...]).astype(bf16)
    own[:, FQ:] = mm_nn(chosen, quarter[...]).astype(bf16)
    wait_entered()

    swap = remote(own, other, core_sem, 0, sibling)
    swap.start()
    half_rows = ROWS // 2

    def share(index, origin, start, count, device):
        part = x_ref.at[pl.ds(start, count), lanes(origin * FQ, FQ)]
        source = points_ref if index < 2 else part
        return remote(source, part, p_sems[index], 0, device)

    share(0, x, 0, ROWS, left).start()
    share(1, x, 0, ROWS, right).start()
    swap.wait()
    mine, theirs = own[...].astype(f32), other[...].astype(f32)
    first = core == 0
    pair = jnp.concatenate(
        [
            jnp.where(first, mine[:MAXP], theirs[MAXP:]),
            jnp.where(first, theirs[:MAXP], mine[MAXP:]),
        ],
        axis=0,
    ).astype(bf16)

    lines, rings = [], []
    for i, (start, width, y_first, _) in enumerate(STREAMS):
        here, there, peers = (z, y, y_peers) if y_first else (y, z, z_peers)
        bufs[i][here, there] = pair[:, start : start + width]
        part = bufs[i].at[here, there]
        lines.append([remote(part, part, line_sems[i], 0, peers[d]) for d in range(NY - 1)])
    for d in (3, 2, 4, 1, 5, 0, 6):
        for line in lines:
            line[d].start()

    counts = jnp.where(first, counts_ref[0:1, :], counts_ref[1:2, :]).astype(f32)
    counts = jnp.broadcast_to(counts, (8, 128)).astype(bf16)
    before = lax.broadcasted_iota(jnp.int32, (128, 128), 0) < lax.broadcasted_iota(
        jnp.int32, (128, 128), 1
    )
    offsets = mm_nn(counts, before.astype(bf16)).astype(bf16)
    owner_row = lax.broadcasted_iota(jnp.int32, (128, 1024), 0)
    column = lax.broadcasted_iota(jnp.int32, (128, 1024), 1)
    slot = (lax.broadcasted_iota(jnp.int32, (8, 1024), 1) % MAXP).astype(f32)
    pivot_row = lax.broadcasted_iota(jnp.int32, (BLOCK, 1024), 0)

    def places(owner_of):
        spread = (owner_row == owner_of(column // MAXP)).astype(bf16)
        start, count = mm_nn(offsets, spread), mm_nn(counts, spread)
        target = jnp.where(slot < count, start + slot, -1.0)
        return (pivot_row.astype(f32) == target[0:1, :]).astype(bf16)

    def swapped(position):
        return ((position // CORES) % NZ * NY + position // (CORES * NZ)) * CORES + position % CORES

    compact = (places(swapped), places(lambda position: position))

    for i, (start, width, y_first, _) in enumerate(STREAMS):
        here, peers = (z, y_peers) if y_first else (y, z_peers)
        seven = bufs[i].at[here, pl.ds(0, NY - 1)]
        remote(seven, seven, line_sems[i], 0, peers[0]).wait()

    def ring(buf, sems, me, count, up, down):
        last = count // 2 - 1
        size = buf.shape[1] // PARTS

        def go_up(step, part, origin):
            piece = buf.at[origin % count, pl.ds(part * size, size)]
            return remote(piece, piece, sems, step * PARTS + part, up)

        def go_down(step, part, origin):
            piece = buf.at[origin % count, pl.ds(part * size, size)]
            return remote(piece, piece, sems, RECEIVED // 2 + step * PARTS + part - (step == last) * PARTS // 2, down)

        goes_up = lambda step, part: step < last or part < PARTS // 2
        goes_down = lambda step, part: step < last or part >= PARTS // 2

        def send(step, part):
            if goes_up(step, part):
                go_up(step, part, me + count - step).start()
            if goes_down(step, part):
                go_down(step, part, me + step).start()

        def receive(step, part):
            if goes_up(step, part):
                go_up(step, part, me + count - 1 - step).wait_recv()
            if goes_down(step, part):
                go_down(step, part, me + 1 + step).wait_recv()

        def finish():
            sent = buf.at[pl.ds(0, count - 1)]
            remote(sent, sent, sems, 0, up).wait_send()

        return send, receive, finish

    for i, (start, width, y_first, _) in enumerate(STREAMS):
        me, peers = (z, z_peers) if y_first else (y, y_peers)
        rings.append(ring(bufs[i], ring_sems[i], me, NZ, peers[0], peers[NZ - 2]))
    pairs = ((0, 1),)

    def go(wave, step):
        for part in range(PARTS):
            for i in pairs[wave]:
                if step:
                    rings[i][1](step - 1, part)
                if step < NZ // 2:
                    rings[i][0](step, part)

    half = BLOCK // 2
    def part(i, origin, at, count=half):
        place = STREAMS[i][3](origin)
        return g_ref.at[core, pl.ds(at * half, count), lanes(place, STREAMS[i][1])]

    def to_right(i, origin, at, index):
        return remote(part(i, origin, at), part(i, origin, at), x_sems[i], index, right)

    def to_left(i, origin, at, index):
        return remote(part(i, origin, at), part(i, origin, at), x_sems[i], 3 + index, left)

    def to_sibling(i, origin, index):
        block = part(i, origin, 0, BLOCK)
        return remote(block, block, k_sems[i], 0, sibling)

    def join(wave):
        for i in pairs[wave]:
            width, y_first = STREAMS[i][1:3]
            rows = bufs[i][...].reshape(1024, width)
            placed = mm_nn(compact[int(y_first)], rows).astype(bf16)
            g_ref[core, :, lanes(STREAMS[i][3](x), width)] = placed
        for i in pairs[wave]:
            to_right(i, x, 0, 0).start()
            to_left(i, x, 1, 0).start()
        for i in pairs[wave]:
            to_right(i, x, 1, 1).start()
            to_left(i, x, 0, 1).start()
            to_sibling(i, x, 0).start()

    def forward(wave):
        for i in pairs[wave]:
            to_right(i, x_left, 0, 0).wait_recv()
            to_right(i, x_left, 0, 2).start()
            to_left(i, x_right, 1, 0).wait_recv()
            to_left(i, x_right, 1, 2).start()

    def collect(wave):
        for i in pairs[wave]:
            to_right(i, x_left, 1, 1).wait_recv()
            to_sibling(i, x_left, 1).start()
            to_left(i, x_right, 0, 1).wait_recv()
            to_sibling(i, x_right, 2).start()

    def close(wave):
        for i in pairs[wave]:
            to_right(i, x_far, 0, 2).wait_recv()
            to_left(i, x_far, 1, 2).wait_recv()
            to_sibling(i, x_far, 3).start()

    for step in range(NZ // 2 + 1):
        go(0, step)
        if step == 2:
            share(0, x_right, 0, ROWS, left).wait_recv()
            share(2, x_right, 0, half_rows, left).start()
            share(1, x_left, 0, ROWS, right).wait_recv()
            share(3, x_left, half_rows, half_rows, right).start()
    join(0)
    forward(0)
    collect(0)
    close(0)
    for i, (start, width, y_first, _) in enumerate(STREAMS):
        rings[i][2]()
        three = g_ref.at[core, :, lanes(0, 3 * width)]
        remote(three, three, x_sems[i], 0, right).wait_send()
        four = g_ref.at[core, :, lanes(0, 4 * width)]
        remote(four, four, k_sems[i], 0, sibling).wait()
    share(2, x_far, 0, half_rows, left).wait_recv()
    share(3, x_far, half_rows, half_rows, right).wait_recv()
    share(0, x, 0, ROWS, left).wait_send()
    share(1, x, 0, ROWS, right).wait_send()
    share(2, x_right, 0, half_rows, left).wait_send()
    share(3, x_left, half_rows, half_rows, right).wait_send()


def gather_pivots(slots, counts, points, factor):
    vmem = pl.BlockSpec(memory_space=pltpu.VMEM)
    hbm = pl.BlockSpec(memory_space=pltpu.HBM)
    sems = lambda count: pltpu.SemaphoreType.DMA((1 + count,))
    each = len(STREAMS)
    return pl.pallas_call(
        gather_kernel,
        in_specs=[vmem, vmem, hbm, hbm],
        out_specs=[vmem, hbm],
        out_shape=(
            jax.ShapeDtypeStruct((2, BLOCK, NX * W), bf16),
            jax.ShapeDtypeStruct((ROWS, F), bf16),
        ),
        scratch_shapes=[
            pltpu.VMEM((ROWS, FQ), bf16),
            pltpu.VMEM((ROWS, KQ), bf16),
            pltpu.VMEM((2 * MAXP, W), bf16),
            pltpu.VMEM((2 * MAXP, W), bf16),
            pltpu.SemaphoreType.DMA((2,)),
            sems(1),
            *[sems(1)] * 4,
            *[pltpu.VMEM((NZ, NY, 2 * MAXP, stream[1]), bf16) for stream in STREAMS],
            *[sems(1)] * each,
            *[sems(RECEIVED)] * each,
            *[sems(6)] * each,
            *[sems(1)] * each,
        ],
        compiler_params=pltpu.CompilerParams(
            collective_id=0, has_side_effects=True, vmem_limit_bytes=60 * 2**20
        ),
        name="pivot_gather",
    )(slots, counts, points, factor)


def sum_kernel(
    coef_ref, out_ref, got, total, rounded, got_z, piece, got_y, final, core_sem, z_sem, y_sem,
):
    z, y, core = spot()
    sibling = row_id(z, y, 1 - core)
    z_peers = [row_id((z + d) % NZ, y, core) for d in range(1, NZ)]
    y_same = [row_id(z, (y + d) % NY, core) for d in range(1, NY)]
    y_other = [row_id(z, (y + d) % NY, 1 - core) for d in range(NY)]
    enter(z_peers + y_same + y_other)()

    swap = remote(coef_ref.at[1 - core], got, core_sem, 0, sibling)
    swap.start()
    swap.wait()
    total[...] = (coef_ref[core] + got[...]).reshape(NZ, 32, 128)
    rounded[...] = total[...].astype(bf16)
    for d in (3, 2, 4, 1, 5, 0, 6):
        remote(rounded.at[(z + d + 1) % NZ], got_z.at[d], z_sem, 0, z_peers[d]).start()
    remote(rounded.at[pl.ds(0, NZ - 1)], got_z, z_sem, 0, z_peers[0]).wait()
    mine = total[z]
    for d in range(NZ - 1):
        mine = mine + got_z[d].astype(f32)
    piece[...] = mine.reshape(4, 8, 128)
    for d in (4, 3, 5, 2, 6, 1, 7, 0):
        tile = piece.at[(y + d) % NY // 2]
        if d:
            remote(tile, got_y.at[core, d], y_sem, 0, y_same[d - 1]).start()
        remote(tile, got_y.at[core, d], y_sem, 1, y_other[d]).start()
    same, cross = got_y.at[core, pl.ds(1, NY - 1)], got_y.at[1 - core]
    remote(same, same, y_sem, 0, y_same[0]).wait()
    remote(cross, cross, y_sem, 1, y_other[0]).wait()
    got_y[core, 0] = piece[y // 2]
    for b in range(2):
        mine = got_y[b, 0]
        for d in range(1, NY):
            mine = mine + got_y[b, d]
        final[b] = mine
    at = (y % 2) * 4 + core * 2
    out_ref[0] = final[0, pl.ds(at, 2), :]
    out_ref[1] = final[1, pl.ds(at, 2), :]


def sum_coefficients(coef):
    vmem = pl.BlockSpec(memory_space=pltpu.VMEM)
    sems = lambda count: pltpu.SemaphoreType.DMA((1 + count,))
    return pl.pallas_call(
        sum_kernel,
        in_specs=[vmem],
        out_specs=vmem,
        out_shape=jax.ShapeDtypeStruct((2, 2, 128), f32),
        scratch_shapes=[
            pltpu.VMEM((BLOCK, 128), f32),
            pltpu.VMEM((NZ, 32, 128), f32),
            pltpu.VMEM((NZ, 32, 128), bf16),
            pltpu.VMEM((NZ - 1, 32, 128), bf16),
            pltpu.VMEM((4, 8, 128), f32),
            pltpu.VMEM((2, NY, 8, 128), f32),
            pltpu.VMEM((2, 8, 128), f32),
            sems(1),
            sems(1),
            sems(2),
        ],
        compiler_params=pltpu.CompilerParams(collective_id=1, has_side_effects=True),
        name="coefficient_sum",
    )(coef)


def local(points, factor, targets, pivot_slots, pivot_counts):
    g, x = gather_pivots(pivot_slots, pivot_counts, points, factor)
    new, res, coef = solve_rows(g, points, x, factor, targets)
    return jnp.swapaxes(new, 1, 2), res, sum_coefficients(coef)


def solution(mesh):
    in_specs = (P("rows", "cols"), P("rows", None), P("rows", "cols"), P(None, "rows"), P())
    out_specs = (P(None, "rows", "cols"), P(None, "rows"), P(None, "rows", "cols"))
    return jax.shard_map(local, mesh=mesh, in_specs=in_specs, out_specs=out_specs, check_vma=False)
```

```python
import functools
import jax
import jax.numpy as jnp
from jax import lax
from jax.experimental import pallas as pl
from jax.experimental.pallas import tpu as pltpu
from jax.sharding import PartitionSpec as P

F = 1024
BLOCK = 256
MAXP = 8
NX = 4
FQ = 256
KQ = 384
W = FQ + KQ
ROWS = 1024
TILE = 256
HI = lax.Precision.HIGHEST
f32 = jnp.float32
bf16 = jnp.bfloat16


def mm_nt(a, b, precision=None):
    return lax.dot_general(
        a, b, (((1,), (1,)), ((), ())), precision=precision, preferred_element_type=f32
    )


def mm_nn(a, b, precision=None):
    return lax.dot_general(
        a, b, (((1,), (0,)), ((), ())), precision=precision, preferred_element_type=f32
    )


def mm_tn(a, b):
    return lax.dot_general(a, b, (((0,), (0,)), ((), ())), preferred_element_type=f32)


def split2(a):
    high = a.astype(bf16)
    return high, (a - high.astype(f32)).astype(bf16)


def nothing():
    pass


def chol_inv_128(a, beside=()):
    n = 16
    beside = list(beside)
    sub = lax.broadcasted_iota(jnp.int32, (8, 128), 0)
    lane = lax.broadcasted_iota(jnp.int32, (8, 128), 1)
    A = [a[8 * r : 8 * r + 8, :] for r in range(n)]
    X = [jnp.where(lane == sub + 8 * r, 1.0, 0.0).astype(f32) for r in range(n)]
    row = lambda v, j: jnp.broadcast_to(v[j : j + 1, :], (8, 128))
    out = []
    for k in range(n):
        columns = lambda v: [
            jnp.broadcast_to(v[:, 8 * k + m : 8 * k + m + 1], (8, 128)) for m in range(8)
        ]
        panel, own_a, own_x = columns(A[k]), A[k], X[k]
        pivots = jnp.ones((8, 128), f32)
        steps = []
        for j in range(8):
            row_p = [row(panel[m], j) if m >= j else None for m in range(8)]
            inverse = 1.0 / row_p[j]
            below = jnp.where(sub > j, panel[j], 0.0)
            for m in range(j + 1, 8):
                panel[m] = panel[m] - (below * row_p[m]) * inverse
            row_a, row_x = row(own_a, j), row(own_x, j)
            steps.append((row_a, row_x, row_p, inverse))
            pivots = jnp.where(sub == j, row_p[j], pivots)
            c = below * inverse
            own_a = own_a - c * row_a
            own_x = own_x - c * row_x
        out.append(own_x * lax.rsqrt(pivots))
        for r in range(k + 1, n):
            part = columns(A[r])
            for j, (row_a, row_x, row_p, inverse) in enumerate(steps):
                c = part[j] * inverse
                A[r] = A[r] - c * row_a
                X[r] = X[r] - c * row_x
                for m in range(j + 1, 8):
                    part[m] = part[m] - c * row_p[m]
        due = (len(beside) + n - 2 - k) // (n - 1 - k) if k < n - 1 else len(beside)
        for work in beside[:due]:
            work()
        beside = beside[due:]
    return jnp.concatenate(out, axis=0)


def chol_inv_256(a, beside=((), ())):
    inv11 = chol_inv_128(a[:128, :128], beside[0])
    low21 = mm_nt(a[128:, :128], inv11, HI)
    inv22 = chol_inv_128(a[128:, 128:] - mm_nt(low21, low21, HI), beside[1])
    inv21 = -mm_nn(inv22, mm_nn(low21, inv11, HI), HI)
    zero = jnp.zeros((128, 128), f32)
    return jnp.concatenate(
        [jnp.concatenate([inv11, zero], axis=1), jnp.concatenate([inv21, inv22], axis=1)], axis=0
    )


def lanes(start, width):
    return pl.ds(pl.multiple_of(start, 128), width)


def fold(v):
    total = v[:, :128]
    for i in range(1, v.shape[1] // 128):
        total = total + v[:, 128 * i : 128 * i + 128]
    return total


def across(v):
    return jnp.sum(jnp.transpose(v), axis=0, keepdims=True)


def solve_kernel(
    g_hbm, p_hbm, x_hbm, f_hbm, t_hbm, new_ref, res_ref, coef_ref,
    g_ref, x_ref, f_ref, t_ref, columns, solved, narrow, squares, block10, block11, sems,
):
    place = lax.axis_index("cols")
    loads = [
        pltpu.make_async_copy(g_hbm.at[0], g_ref.at[0], sems.at[0]),
        pltpu.make_async_copy(g_hbm.at[1], g_ref.at[1], sems.at[1]),
        pltpu.make_async_copy(f_hbm, f_ref, sems.at[2]),
        pltpu.make_async_copy(t_hbm, t_ref, sems.at[3]),
        pltpu.make_async_copy(p_hbm, x_ref.at[:, lanes(place * FQ, FQ)], sems.at[4]),
    ]
    for d in range(1, NX):
        part = lanes((place + d) % NX * FQ, FQ)
        loads.append(pltpu.make_async_copy(x_hbm.at[:, part], x_ref.at[:, part], sems.at[4 + d]))
    for load in loads:
        load.start()
    eye = lax.broadcasted_iota(jnp.int32, (BLOCK, BLOCK), 0) == lax.broadcasted_iota(
        jnp.int32, (BLOCK, BLOCK), 1
    )

    def gram(a, b):
        dots = mm_nt(g_ref[a, :, :F], g_ref[b, :, :F])
        return dots, mm_nt(g_ref[a, :, F:], g_ref[b, :, F:])

    def kernel_matrix(col, row, dots, basis):
        return jnp.exp(-(col + row - 2.0 * dots) / F) - basis

    loads[0].wait()
    dots00, basis00 = gram(0, 0)
    diag = jnp.where(eye, dots00, 0.0)
    col0, row0 = jnp.sum(diag, axis=1, keepdims=True), jnp.sum(diag, axis=0, keepdims=True)
    a00 = kernel_matrix(col0, row0, dots00, basis00)

    cols = [col0, None]

    def tile(t):
        return pl.ds(t * TILE, TILE)

    def norms(t):
        def work():
            squares[0, :, tile(t)] = across(fold(jnp.square(x_ref[tile(t), :].astype(f32))))
            res_ref[0:1, tile(t)] = 1.0 - across(fold(jnp.square(f_ref[tile(t), :].astype(f32))))
        return work

    def fill(b, t):
        def work():
            dots = mm_nt(g_ref[b, :, :F], x_ref[tile(t), :])
            basis = mm_nt(g_ref[b, :, F:], f_ref[tile(t), :])
            columns[b, :, tile(t)] = kernel_matrix(cols[b], squares[0, :, tile(t)], dots, basis)
        return work

    def solve(b, inverse, t):
        high, low = split2(columns[b, :, tile(t)])
        fresh = mm_nn(inverse[0], high) + mm_nn(inverse[1], high) + mm_nn(inverse[0], low)
        solved[:, tile(t)] = fresh
        narrow[:, tile(t)] = fresh.astype(bf16)
        before = res_ref[0:1, tile(t)]
        res_ref[b : b + 1, tile(t)] = before - jnp.sum(jnp.square(fresh), axis=0, keepdims=True)

    tiles = range(ROWS // TILE)

    def later():
        for load in loads[1:]:
            load.wait()
        dots, basis = gram(1, 1)
        diag = jnp.where(eye, dots, 0.0)
        cols[1] = jnp.sum(diag, axis=1, keepdims=True)
        row1 = jnp.sum(diag, axis=0, keepdims=True)
        block11[...] = kernel_matrix(cols[1], row1, dots, basis)
        dots, basis = gram(1, 0)
        block10[...] = kernel_matrix(cols[1], row0, dots, basis)

    inv0 = chol_inv_256(
        a00,
        (
            [nothing] * 5 + [later] + [norms(t) for t in tiles],
            [fill(b, t) for b in range(2) for t in tiles],
        ),
    )
    split0 = split2(inv0)
    narrow10 = mm_nt(block10[...], inv0, HI).astype(bf16)
    a11 = block11[...] - mm_nt(narrow10, narrow10)

    def apply0(t):
        def work():
            solve(0, split0, t)
            columns[1, :, tile(t)] = columns[1, :, tile(t)] - mm_nn(narrow10, narrow[:, tile(t)])
        return work

    def emit(b):
        def work():
            new_ref[b] = solved[pl.ds(pl.multiple_of(place * 64, 64), 64), :]
        return work

    def coefficients(b):
        def work():
            coef_ref[b] = mm_nn(narrow[...], t_ref[...])
        return work

    inv1 = chol_inv_256(a11, ([apply0(t) for t in tiles], [emit(0), coefficients(0)]))
    split1 = split2(inv1)
    for t in tiles:
        solve(1, split1, t)
    coefficients(1)()
    emit(1)()


def solve_rows(g, points, x, factor, targets):
    any_ = pl.BlockSpec(memory_space=pl.ANY)
    vmem = pl.BlockSpec(memory_space=pltpu.VMEM)
    return pl.pallas_call(
        solve_kernel,
        in_specs=[any_] * 5,
        out_specs=[vmem] * 3,
        out_shape=(
            jax.ShapeDtypeStruct((2, 64, ROWS), f32),
            jax.ShapeDtypeStruct((2, ROWS), f32),
            jax.ShapeDtypeStruct((2, BLOCK, 128), f32),
        ),
        scratch_shapes=[
            pltpu.VMEM((2, BLOCK, NX * W), bf16),
            pltpu.VMEM((ROWS, F), bf16),
            pltpu.VMEM((ROWS, NX * KQ), bf16),
            pltpu.VMEM((ROWS, 128), bf16),
            pltpu.VMEM((2, BLOCK, ROWS), f32),
            pltpu.VMEM((BLOCK, ROWS), f32),
            pltpu.VMEM((BLOCK, ROWS), bf16),
            pltpu.VMEM((1, 1, ROWS), f32),
            pltpu.VMEM((BLOCK, BLOCK), f32),
            pltpu.VMEM((BLOCK, BLOCK), f32),
            pltpu.SemaphoreType.DMA((8,)),
        ],
        compiler_params=pltpu.CompilerParams(vmem_limit_bytes=60 * 2**20),
        name="pivot_solve",
    )(g, points, x, factor, targets)


NZ = 8
NY = 8
CORES = 2
PARTS = 4
RECEIVED = (NZ - 1) * PARTS
MESH = pl.DeviceIdType.MESH


def spot():
    index = lax.axis_index("rows")
    return index // (NY * CORES), (index // CORES) % NY, index % CORES


def row_id(z, y, core):
    return {"rows": (z * NY + y) * CORES + core}


def enter(devices):
    barrier = pltpu.get_barrier_semaphore()
    for device in devices:
        pl.semaphore_signal(barrier, inc=1, device_id=device, device_id_type=MESH)
    return lambda: pl.semaphore_wait(barrier, len(devices))


def remote(src, dst, sems, index, device):
    return pltpu.make_async_remote_copy(
        src_ref=src,
        dst_ref=dst,
        send_sem=sems.at[0],
        recv_sem=sems.at[1 + index],
        device_id=device,
        device_id_type=MESH,
    )


STREAMS = (
    (0, FQ, False, lambda o: FQ * o),
    (FQ, KQ, True, lambda o: F + KQ * o),
)


def gather_kernel(slots_hbm, counts_hbm, points_ref, factor_ref, g_ref, x_ref, *scratch):
    mine_points, quarter, own, other, load_sem, core_sem = scratch[:6]
    p_sems = scratch[6:10]
    slots_ref, counts_ref = scratch[10:12]
    n = len(STREAMS)
    bufs, line_sems, ring_sems, x_sems, k_sems = [scratch[12 + n * i : 12 + n + n * i] for i in range(5)]
    z, y, core = spot()
    x = lax.axis_index("cols")
    sibling = row_id(z, y, 1 - core)
    y_peers = [row_id(z, (y + d) % NY, core) for d in range(1, NY)]
    z_peers = [row_id((z + d) % NZ, y, core) for d in range(1, NZ)]
    right, left = {"cols": (x + 1) % NX}, {"cols": (x + NX - 1) % NX}
    x_left, x_right, x_far = (x + NX - 1) % NX, (x + 1) % NX, (x + 2) % NX

    wait_entered = enter([sibling] + y_peers + z_peers + [right, left])
    loads = [
        pltpu.make_async_copy(slots_hbm, slots_ref, load_sem.at[2]),
        pltpu.make_async_copy(counts_hbm, counts_ref, load_sem.at[3]),
        pltpu.make_async_copy(factor_ref.at[:, lanes(x * KQ, KQ)], quarter, load_sem.at[0]),
        pltpu.make_async_copy(points_ref, mine_points, load_sem.at[1]),
    ]
    for load in loads:
        load.start()
    for load in loads[:2]:
        load.wait()

    diagonal = lax.broadcasted_iota(jnp.int32, (MAXP, MAXP), 0) == lax.broadcasted_iota(
        jnp.int32, (MAXP, MAXP), 1
    )
    slots = [
        jnp.sum(
            jnp.where(diagonal, slots_ref[b : b + 1, :].astype(f32), 0.0), axis=1, keepdims=True
        ).astype(jnp.int32)
        for b in range(2)
    ]
    point = lax.broadcasted_iota(jnp.int32, (MAXP, ROWS), 1)
    chosen = jnp.concatenate([(point == slot).astype(f32) for slot in slots], axis=0).astype(bf16)
    for load in loads[2:]:
        load.wait()
    own[:, :FQ] = mm_nn(chosen, mine_points[...]).astype(bf16)
    own[:, FQ:] = mm_nn(chosen, quarter[...]).astype(bf16)
    wait_entered()

    swap = remote(own, other, core_sem, 0, sibling)
    swap.start()
    half_rows = ROWS // 2

    def share(index, origin, start, count, device):
        part = x_ref.at[pl.ds(start, count), lanes(origin * FQ, FQ)]
        source = points_ref if index < 2 else part
        return remote(source, part, p_sems[index], 0, device)

    share(0, x, 0, ROWS, left).start()
    share(1, x, 0, ROWS, right).start()
    swap.wait()
    mine, theirs = own[...].astype(f32), other[...].astype(f32)
    first = core == 0
    pair = jnp.concatenate(
        [
            jnp.where(first, mine[:MAXP], theirs[MAXP:]),
            jnp.where(first, theirs[:MAXP], mine[MAXP:]),
        ],
        axis=0,
    ).astype(bf16)

    lines, rings = [], []
    for i, (start, width, y_first, _) in enumerate(STREAMS):
        here, there, peers = (z, y, y_peers) if y_first else (y, z, z_peers)
        bufs[i][here, there] = pair[:, start : start + width]
        part = bufs[i].at[here, there]
        lines.append([remote(part, part, line_sems[i], 0, peers[d]) for d in range(NY - 1)])
    for d in (3, 2, 4, 1, 5, 0, 6):
        for line in lines:
            line[d].start()

    counts = jnp.where(first, counts_ref[0:1, :], counts_ref[1:2, :]).astype(f32)
    counts = jnp.broadcast_to(counts, (8, 128)).astype(bf16)
    before = lax.broadcasted_iota(jnp.int32, (128, 128), 0) < lax.broadcasted_iota(
        jnp.int32, (128, 128), 1
    )
    offsets = mm_nn(counts, before.astype(bf16)).astype(bf16)
    owner_row = lax.broadcasted_iota(jnp.int32, (128, 1024), 0)
    column = lax.broadcasted_iota(jnp.int32, (128, 1024), 1)
    slot = (lax.broadcasted_iota(jnp.int32, (8, 1024), 1) % MAXP).astype(f32)
    pivot_row = lax.broadcasted_iota(jnp.int32, (BLOCK, 1024), 0)

    def places(owner_of):
        spread = (owner_row == owner_of(column // MAXP)).astype(bf16)
        start, count = mm_nn(offsets, spread), mm_nn(counts, spread)
        target = jnp.where(slot < count, start + slot, -1.0)
        return (pivot_row.astype(f32) == target[0:1, :]).astype(bf16)

    def swapped(position):
        return ((position // CORES) % NZ * NY + position // (CORES * NZ)) * CORES + position % CORES

    compact = (places(swapped), places(lambda position: position))

    for i, (start, width, y_first, _) in enumerate(STREAMS):
        here, peers = (z, y_peers) if y_first else (y, z_peers)
        seven = bufs[i].at[here, pl.ds(0, NY - 1)]
        remote(seven, seven, line_sems[i], 0, peers[0]).wait()

    def ring(buf, sems, me, count, up, down):
        last = count // 2 - 1
        size = buf.shape[1] // PARTS

        def go_up(step, part, origin):
            piece = buf.at[origin % count, pl.ds(part * size, size)]
            return remote(piece, piece, sems, step * PARTS + part, up)

        def go_down(step, part, origin):
            piece = buf.at[origin % count, pl.ds(part * size, size)]
            return remote(piece, piece, sems, RECEIVED // 2 + step * PARTS + part - (step == last) * PARTS // 2, down)

        goes_up = lambda step, part: step < last or part < PARTS // 2
        goes_down = lambda step, part: step < last or part >= PARTS // 2

        def send(step, part):
            if goes_up(step, part):
                go_up(step, part, me + count - step).start()
            if goes_down(step, part):
                go_down(step, part, me + step).start()

        def receive(step, part):
            if goes_up(step, part):
                go_up(step, part, me + count - 1 - step).wait_recv()
            if goes_down(step, part):
                go_down(step, part, me + 1 + step).wait_recv()

        def finish():
            sent = buf.at[pl.ds(0, count - 1)]
            remote(sent, sent, sems, 0, up).wait_send()

        return send, receive, finish

    for i, (start, width, y_first, _) in enumerate(STREAMS):
        me, peers = (z, z_peers) if y_first else (y, y_peers)
        rings.append(ring(bufs[i], ring_sems[i], me, NZ, peers[0], peers[NZ - 2]))
    pairs = ((0, 1),)

    def go(wave, step):
        for part in range(PARTS):
            for i in pairs[wave]:
                if step:
                    rings[i][1](step - 1, part)
                if step < NZ // 2:
                    rings[i][0](step, part)

    half = BLOCK // 2
    def part(i, origin, at, count=half):
        place = STREAMS[i][3](origin)
        return g_ref.at[core, pl.ds(at * half, count), lanes(place, STREAMS[i][1])]

    def to_right(i, origin, at, index):
        return remote(part(i, origin, at), part(i, origin, at), x_sems[i], index, right)

    def to_left(i, origin, at, index):
        return remote(part(i, origin, at), part(i, origin, at), x_sems[i], 3 + index, left)

    def to_sibling(i, origin, index):
        block = part(i, origin, 0, BLOCK)
        return remote(block, block, k_sems[i], 0, sibling)

    def join(wave):
        for i in pairs[wave]:
            width, y_first = STREAMS[i][1:3]
            rows = bufs[i][...].reshape(1024, width)
            placed = mm_nn(compact[int(y_first)], rows).astype(bf16)
            g_ref[core, :, lanes(STREAMS[i][3](x), width)] = placed
            to_right(i, x, 0, 0).start()
            to_left(i, x, 1, 0).start()
        for i in pairs[wave]:
            to_right(i, x, 1, 1).start()
            to_left(i, x, 0, 1).start()
            to_sibling(i, x, 0).start()

    def forward(wave):
        for i in pairs[wave]:
            to_right(i, x_left, 0, 0).wait_recv()
            to_right(i, x_left, 0, 2).start()
            to_left(i, x_right, 1, 0).wait_recv()
            to_left(i, x_right, 1, 2).start()

    def collect(wave):
        for i in pairs[wave]:
            to_right(i, x_left, 1, 1).wait_recv()
            to_sibling(i, x_left, 1).start()
            to_left(i, x_right, 0, 1).wait_recv()
            to_sibling(i, x_right, 2).start()

    def close(wave):
        for i in pairs[wave]:
            to_right(i, x_far, 0, 2).wait_recv()
            to_left(i, x_far, 1, 2).wait_recv()
            to_sibling(i, x_far, 3).start()

    for step in range(NZ // 2 + 1):
        go(0, step)
        if step == 2:
            share(0, x_right, 0, ROWS, left).wait_recv()
            share(2, x_right, 0, half_rows, left).start()
            share(1, x_left, 0, ROWS, right).wait_recv()
            share(3, x_left, half_rows, half_rows, right).start()
    join(0)
    forward(0)
    collect(0)
    close(0)
    for i, (start, width, y_first, _) in enumerate(STREAMS):
        rings[i][2]()
        three = g_ref.at[core, :, lanes(0, 3 * width)]
        remote(three, three, x_sems[i], 0, right).wait_send()
        four = g_ref.at[core, :, lanes(0, 4 * width)]
        remote(four, four, k_sems[i], 0, sibling).wait()
    share(2, x_far, 0, half_rows, left).wait_recv()
    share(3, x_far, half_rows, half_rows, right).wait_recv()
    share(0, x, 0, ROWS, left).wait_send()
    share(1, x, 0, ROWS, right).wait_send()
    share(2, x_right, 0, half_rows, left).wait_send()
    share(3, x_left, half_rows, half_rows, right).wait_send()


def gather_pivots(slots, counts, points, factor):
    vmem = pl.BlockSpec(memory_space=pltpu.VMEM)
    hbm = pl.BlockSpec(memory_space=pltpu.HBM)
    sems = lambda count: pltpu.SemaphoreType.DMA((1 + count,))
    each = len(STREAMS)
    return pl.pallas_call(
        gather_kernel,
        in_specs=[hbm] * 4,
        out_specs=[vmem, hbm],
        out_shape=(
            jax.ShapeDtypeStruct((2, BLOCK, NX * W), bf16),
            jax.ShapeDtypeStruct((ROWS, F), bf16),
        ),
        scratch_shapes=[
            pltpu.VMEM((ROWS, FQ), bf16),
            pltpu.VMEM((ROWS, KQ), bf16),
            pltpu.VMEM((2 * MAXP, W), bf16),
            pltpu.VMEM((2 * MAXP, W), bf16),
            pltpu.SemaphoreType.DMA((4,)),
            sems(1),
            *[sems(1)] * 4,
            pltpu.VMEM((2, MAXP), jnp.int32),
            pltpu.VMEM((2, 128), jnp.int32),
            *[pltpu.VMEM((NZ, NY, 2 * MAXP, stream[1]), bf16) for stream in STREAMS],
            *[sems(1)] * each,
            *[sems(RECEIVED)] * each,
            *[sems(6)] * each,
            *[sems(1)] * each,
        ],
        compiler_params=pltpu.CompilerParams(
            collective_id=0, has_side_effects=True, vmem_limit_bytes=60 * 2**20
        ),
        name="pivot_gather",
    )(slots, counts, points, factor)


def sum_kernel(
    coef_ref, out_ref, mine_coef, load_sem, got, total, rounded, got_z, piece, got_y, final, core_sem, z_sem, y_sem,
):
    z, y, core = spot()
    sibling = row_id(z, y, 1 - core)
    z_peers = [row_id((z + d) % NZ, y, core) for d in range(1, NZ)]
    y_same = [row_id(z, (y + d) % NY, core) for d in range(1, NY)]
    y_other = [row_id(z, (y + d) % NY, 1 - core) for d in range(NY)]
    wait_entered = enter(z_peers + y_same + y_other)
    load = pltpu.make_async_copy(coef_ref.at[core], mine_coef, load_sem)
    load.start()
    load.wait()
    wait_entered()

    swap = remote(coef_ref.at[1 - core], got, core_sem, 0, sibling)
    swap.start()
    swap.wait()
    total[...] = (mine_coef[...] + got[...]).reshape(NZ, 32, 128)
    rounded[...] = total[...].astype(bf16)
    for d in (3, 2, 4, 1, 5, 0, 6):
        remote(rounded.at[(z + d + 1) % NZ], got_z.at[d], z_sem, 0, z_peers[d]).start()
    remote(rounded.at[pl.ds(0, NZ - 1)], got_z, z_sem, 0, z_peers[0]).wait()
    mine = total[z]
    for d in range(NZ - 1):
        mine = mine + got_z[d].astype(f32)
    piece[...] = mine.reshape(4, 8, 128)
    for d in (4, 3, 5, 2, 6, 1, 7, 0):
        tile = piece.at[(y + d) % NY // 2]
        if d:
            remote(tile, got_y.at[core, d], y_sem, 0, y_same[d - 1]).start()
        remote(tile, got_y.at[core, d], y_sem, 1, y_other[d]).start()
    same, cross = got_y.at[core, pl.ds(1, NY - 1)], got_y.at[1 - core]
    remote(same, same, y_sem, 0, y_same[0]).wait()
    remote(cross, cross, y_sem, 1, y_other[0]).wait()
    got_y[core, 0] = piece[y // 2]
    for b in range(2):
        mine = got_y[b, 0]
        for d in range(1, NY):
            mine = mine + got_y[b, d]
        final[b] = mine
    at = (y % 2) * 4 + core * 2
    out_ref[0] = final[0, pl.ds(at, 2), :]
    out_ref[1] = final[1, pl.ds(at, 2), :]


def sum_coefficients(coef):
    vmem = pl.BlockSpec(memory_space=pltpu.VMEM)
    sems = lambda count: pltpu.SemaphoreType.DMA((1 + count,))
    return pl.pallas_call(
        sum_kernel,
        in_specs=[pl.BlockSpec(memory_space=pl.ANY)],
        out_specs=vmem,
        out_shape=jax.ShapeDtypeStruct((2, 2, 128), f32),
        scratch_shapes=[
            pltpu.VMEM((BLOCK, 128), f32),
            pltpu.SemaphoreType.DMA,
            pltpu.VMEM((BLOCK, 128), f32),
            pltpu.VMEM((NZ, 32, 128), f32),
            pltpu.VMEM((NZ, 32, 128), bf16),
            pltpu.VMEM((NZ - 1, 32, 128), bf16),
            pltpu.VMEM((4, 8, 128), f32),
            pltpu.VMEM((2, NY, 8, 128), f32),
            pltpu.VMEM((2, 8, 128), f32),
            sems(1),
            sems(1),
            sems(2),
        ],
        compiler_params=pltpu.CompilerParams(
            collective_id=1, has_side_effects=True, vmem_limit_bytes=63 * 2**20 + 2**19
        ),
        name="coefficient_sum",
    )(coef)


def local(points, factor, targets, pivot_slots, pivot_counts):
    g, x = gather_pivots(pivot_slots, pivot_counts, points, factor)
    new, res, coef = solve_rows(g, points, x, factor, targets)
    return jnp.swapaxes(new, 1, 2), res, sum_coefficients(coef)


def solution(mesh):
    in_specs = (P("rows", "cols"), P("rows", None), P("rows", "cols"), P(None, "rows"), P())
    out_specs = (P(None, "rows", "cols"), P(None, "rows"), P(None, "rows", "cols"))
    return jax.shard_map(local, mesh=mesh, in_specs=in_specs, out_specs=out_specs, check_vma=False)
```

```python
import functools
import jax
import jax.numpy as jnp
from jax import lax
from jax.experimental import pallas as pl
from jax.experimental.pallas import tpu as pltpu
from jax.sharding import PartitionSpec as P

F = 1024
BLOCK = 256
MAXP = 8
NX = 4
FQ = 256
KQ = 384
W = FQ + KQ
ROWS = 1024
TILE = 256
HI = lax.Precision.HIGHEST
f32 = jnp.float32
bf16 = jnp.bfloat16


def mm_nt(a, b, precision=None):
    return lax.dot_general(
        a, b, (((1,), (1,)), ((), ())), precision=precision, preferred_element_type=f32
    )


def mm_nn(a, b, precision=None):
    return lax.dot_general(
        a, b, (((1,), (0,)), ((), ())), precision=precision, preferred_element_type=f32
    )


def mm_tn(a, b):
    return lax.dot_general(a, b, (((0,), (0,)), ((), ())), preferred_element_type=f32)


def split2(a):
    high = a.astype(bf16)
    return high, (a - high.astype(f32)).astype(bf16)


def nothing():
    pass


def chol_inv_128(a, beside=()):
    n = 16
    beside = list(beside)
    sub = lax.broadcasted_iota(jnp.int32, (8, 128), 0)
    lane = lax.broadcasted_iota(jnp.int32, (8, 128), 1)
    A = [a[8 * r : 8 * r + 8, :] for r in range(n)]
    X = [jnp.where(lane == sub + 8 * r, 1.0, 0.0).astype(f32) for r in range(n)]
    row = lambda v, j: jnp.broadcast_to(v[j : j + 1, :], (8, 128))
    out = []
    for k in range(n):
        columns = lambda v: [
            jnp.broadcast_to(v[:, 8 * k + m : 8 * k + m + 1], (8, 128)) for m in range(8)
        ]
        panel, own_a, own_x = columns(A[k]), A[k], X[k]
        pivots = jnp.ones((8, 128), f32)
        steps = []
        for j in range(8):
            row_p = [row(panel[m], j) if m >= j else None for m in range(8)]
            inverse = 1.0 / row_p[j]
            below = jnp.where(sub > j, panel[j], 0.0)
            for m in range(j + 1, 8):
                panel[m] = panel[m] - (below * row_p[m]) * inverse
            row_a, row_x = row(own_a, j), row(own_x, j)
            steps.append((row_a, row_x, row_p, inverse))
            pivots = jnp.where(sub == j, row_p[j], pivots)
            c = below * inverse
            own_a = own_a - c * row_a
            own_x = own_x - c * row_x
        out.append(own_x * lax.rsqrt(pivots))
        for r in range(k + 1, n):
            part = columns(A[r])
            for j, (row_a, row_x, row_p, inverse) in enumerate(steps):
                c = part[j] * inverse
                A[r] = A[r] - c * row_a
                X[r] = X[r] - c * row_x
                for m in range(j + 1, 8):
                    part[m] = part[m] - c * row_p[m]
        due = (len(beside) + n - 2 - k) // (n - 1 - k) if k < n - 1 else len(beside)
        for work in beside[:due]:
            work()
        beside = beside[due:]
    return jnp.concatenate(out, axis=0)


def chol_inv_256(a, beside=((), ())):
    inv11 = chol_inv_128(a[:128, :128], beside[0])
    low21 = mm_nt(a[128:, :128], inv11, HI)
    inv22 = chol_inv_128(a[128:, 128:] - mm_nt(low21, low21, HI), beside[1])
    inv21 = -mm_nn(inv22, mm_nn(low21, inv11, HI), HI)
    zero = jnp.zeros((128, 128), f32)
    return jnp.concatenate(
        [jnp.concatenate([inv11, zero], axis=1), jnp.concatenate([inv21, inv22], axis=1)], axis=0
    )


def lanes(start, width):
    return pl.ds(pl.multiple_of(start, 128), width)


def fold(v):
    total = v[:, :128]
    for i in range(1, v.shape[1] // 128):
        total = total + v[:, 128 * i : 128 * i + 128]
    return total


def across(v):
    return jnp.sum(jnp.transpose(v), axis=0, keepdims=True)


def solve_kernel(
    g_hbm, p_hbm, x_hbm, f_hbm, t_hbm, new_ref, res_ref, coef_ref,
    g_ref, x_ref, f_ref, t_ref, columns, solved, narrow, squares, block10, block11, sems,
):
    place = lax.axis_index("cols")
    loads = [
        pltpu.make_async_copy(g_hbm.at[0], g_ref.at[0], sems.at[0]),
        pltpu.make_async_copy(g_hbm.at[1], g_ref.at[1], sems.at[1]),
        pltpu.make_async_copy(f_hbm, f_ref, sems.at[2]),
        pltpu.make_async_copy(t_hbm, t_ref, sems.at[3]),
        pltpu.make_async_copy(p_hbm, x_ref.at[:, lanes(place * FQ, FQ)], sems.at[4]),
    ]
    for d in range(1, NX):
        part = lanes((place + d) % NX * FQ, FQ)
        loads.append(pltpu.make_async_copy(x_hbm.at[:, part], x_ref.at[:, part], sems.at[4 + d]))
    for load in loads:
        load.start()
    eye = lax.broadcasted_iota(jnp.int32, (BLOCK, BLOCK), 0) == lax.broadcasted_iota(
        jnp.int32, (BLOCK, BLOCK), 1
    )

    def gram(a, b):
        dots = mm_nt(g_ref[a, :, :F], g_ref[b, :, :F])
        return dots, mm_nt(g_ref[a, :, F:], g_ref[b, :, F:])

    def kernel_matrix(col, row, dots, basis):
        return jnp.exp(-(col + row - 2.0 * dots) / F) - basis

    loads[0].wait()
    dots00, basis00 = gram(0, 0)
    diag = jnp.where(eye, dots00, 0.0)
    col0, row0 = jnp.sum(diag, axis=1, keepdims=True), jnp.sum(diag, axis=0, keepdims=True)
    a00 = kernel_matrix(col0, row0, dots00, basis00)

    cols = [col0, None]

    def tile(t):
        return pl.ds(t * TILE, TILE)

    def norms(t):
        def work():
            squares[0, :, tile(t)] = across(fold(jnp.square(x_ref[tile(t), :].astype(f32))))
            res_ref[0:1, tile(t)] = 1.0 - across(fold(jnp.square(f_ref[tile(t), :].astype(f32))))
        return work

    def fill(b, t):
        def work():
            dots = mm_nt(g_ref[b, :, :F], x_ref[tile(t), :])
            basis = mm_nt(g_ref[b, :, F:], f_ref[tile(t), :])
            columns[b, :, tile(t)] = kernel_matrix(cols[b], squares[0, :, tile(t)], dots, basis)
        return work

    def solve(b, inverse, t):
        high, low = split2(columns[b, :, tile(t)])
        fresh = mm_nn(inverse[0], high) + mm_nn(inverse[1], high) + mm_nn(inverse[0], low)
        solved[:, tile(t)] = fresh
        narrow[:, tile(t)] = fresh.astype(bf16)
        before = res_ref[0:1, tile(t)]
        res_ref[b : b + 1, tile(t)] = before - jnp.sum(jnp.square(fresh), axis=0, keepdims=True)

    tiles = range(ROWS // TILE)

    def later():
        for load in loads[1:]:
            load.wait()
        dots, basis = gram(1, 1)
        diag = jnp.where(eye, dots, 0.0)
        cols[1] = jnp.sum(diag, axis=1, keepdims=True)
        row1 = jnp.sum(diag, axis=0, keepdims=True)
        block11[...] = kernel_matrix(cols[1], row1, dots, basis)
        dots, basis = gram(1, 0)
        block10[...] = kernel_matrix(cols[1], row0, dots, basis)

    inv0 = chol_inv_256(
        a00,
        (
            [nothing] * 5 + [later] + [norms(t) for t in tiles],
            [fill(b, t) for b in range(2) for t in tiles],
        ),
    )
    split0 = split2(inv0)
    narrow10 = mm_nt(block10[...], inv0, HI).astype(bf16)
    a11 = block11[...] - mm_nt(narrow10, narrow10)

    def apply0(t):
        def work():
            solve(0, split0, t)
            columns[1, :, tile(t)] = columns[1, :, tile(t)] - mm_nn(narrow10, narrow[:, tile(t)])
        return work

    def emit(b):
        def work():
            new_ref[b] = solved[pl.ds(pl.multiple_of(place * 64, 64), 64), :]
        return work

    def coefficients(b):
        def work():
            coef_ref[b] = mm_nn(narrow[...], t_ref[...])
        return work

    inv1 = chol_inv_256(a11, ([apply0(t) for t in tiles], [emit(0), coefficients(0)]))
    split1 = split2(inv1)
    for t in tiles:
        solve(1, split1, t)
    coefficients(1)()
    emit(1)()


def solve_rows(g, points, x, factor, targets):
    any_ = pl.BlockSpec(memory_space=pl.ANY)
    vmem = pl.BlockSpec(memory_space=pltpu.VMEM)
    return pl.pallas_call(
        solve_kernel,
        in_specs=[any_] * 5,
        out_specs=[vmem] * 3,
        out_shape=(
            jax.ShapeDtypeStruct((2, 64, ROWS), f32),
            jax.ShapeDtypeStruct((2, ROWS), f32),
            jax.ShapeDtypeStruct((2, BLOCK, 128), f32),
        ),
        scratch_shapes=[
            pltpu.VMEM((2, BLOCK, NX * W), bf16),
            pltpu.VMEM((ROWS, F), bf16),
            pltpu.VMEM((ROWS, NX * KQ), bf16),
            pltpu.VMEM((ROWS, 128), bf16),
            pltpu.VMEM((2, BLOCK, ROWS), f32),
            pltpu.VMEM((BLOCK, ROWS), f32),
            pltpu.VMEM((BLOCK, ROWS), bf16),
            pltpu.VMEM((1, 1, ROWS), f32),
            pltpu.VMEM((BLOCK, BLOCK), f32),
            pltpu.VMEM((BLOCK, BLOCK), f32),
            pltpu.SemaphoreType.DMA((8,)),
        ],
        compiler_params=pltpu.CompilerParams(vmem_limit_bytes=60 * 2**20),
        name="pivot_solve",
    )(g, points, x, factor, targets)


NZ = 8
NY = 8
CORES = 2
PARTS = 4
RECEIVED = (NZ - 1) * PARTS
MESH = pl.DeviceIdType.MESH


def spot():
    index = lax.axis_index("rows")
    return index // (NY * CORES), (index // CORES) % NY, index % CORES


def row_id(z, y, core):
    return {"rows": (z * NY + y) * CORES + core}


def enter(devices):
    barrier = pltpu.get_barrier_semaphore()
    for device in devices:
        pl.semaphore_signal(barrier, inc=1, device_id=device, device_id_type=MESH)
    return lambda: pl.semaphore_wait(barrier, len(devices))


def remote(src, dst, sems, index, device):
    return pltpu.make_async_remote_copy(
        src_ref=src,
        dst_ref=dst,
        send_sem=sems.at[0],
        recv_sem=sems.at[1 + index],
        device_id=device,
        device_id_type=MESH,
    )


STREAMS = (
    (0, FQ, False, lambda o: FQ * o),
    (FQ, KQ, True, lambda o: F + KQ * o),
)


def gather_kernel(slots_hbm, counts_hbm, points_ref, factor_ref, g_ref, x_ref, *scratch):
    mine_points, quarter, own, other, load_sem, core_sem = scratch[:6]
    p_sems = scratch[6:10]
    slots_ref, counts_ref = scratch[10:12]
    n = len(STREAMS)
    bufs, line_sems, ring_sems, x_sems, k_sems = [scratch[12 + n * i : 12 + n + n * i] for i in range(5)]
    z, y, core = spot()
    x = lax.axis_index("cols")
    sibling = row_id(z, y, 1 - core)
    y_peers = [row_id(z, (y + d) % NY, core) for d in range(1, NY)]
    z_peers = [row_id((z + d) % NZ, y, core) for d in range(1, NZ)]
    right, left = {"cols": (x + 1) % NX}, {"cols": (x + NX - 1) % NX}
    x_left, x_right, x_far = (x + NX - 1) % NX, (x + 1) % NX, (x + 2) % NX

    wait_entered = enter([sibling] + y_peers + z_peers + [right, left])
    loads = [
        pltpu.make_async_copy(slots_hbm, slots_ref, load_sem.at[2]),
        pltpu.make_async_copy(counts_hbm, counts_ref, load_sem.at[3]),
        pltpu.make_async_copy(factor_ref.at[:, lanes(x * KQ, KQ)], quarter, load_sem.at[0]),
        pltpu.make_async_copy(points_ref, mine_points, load_sem.at[1]),
    ]
    for load in loads:
        load.start()
    for load in loads[:2]:
        load.wait()

    diagonal = lax.broadcasted_iota(jnp.int32, (MAXP, MAXP), 0) == lax.broadcasted_iota(
        jnp.int32, (MAXP, MAXP), 1
    )
    slots = [
        jnp.sum(
            jnp.where(diagonal, slots_ref[b : b + 1, :].astype(f32), 0.0), axis=1, keepdims=True
        ).astype(jnp.int32)
        for b in range(2)
    ]
    point = lax.broadcasted_iota(jnp.int32, (MAXP, ROWS), 1)
    chosen = jnp.concatenate([(point == slot).astype(f32) for slot in slots], axis=0).astype(bf16)
    for load in loads[2:]:
        load.wait()
    own[:, :FQ] = mm_nn(chosen, mine_points[...]).astype(bf16)
    own[:, FQ:] = mm_nn(chosen, quarter[...]).astype(bf16)
    wait_entered()

    swap = remote(own, other, core_sem, 0, sibling)
    swap.start()
    half_rows = ROWS // 2

    def share(index, origin, start, count, device):
        part = x_ref.at[pl.ds(start, count), lanes(origin * FQ, FQ)]
        source = points_ref if index < 2 else part
        return remote(source, part, p_sems[index], 0, device)

    share(0, x, 0, ROWS, left).start()
    share(1, x, 0, ROWS, right).start()
    swap.wait()
    mine, theirs = own[...].astype(f32), other[...].astype(f32)
    first = core == 0
    pair = jnp.concatenate(
        [
            jnp.where(first, mine[:MAXP], theirs[MAXP:]),
            jnp.where(first, theirs[:MAXP], mine[MAXP:]),
        ],
        axis=0,
    ).astype(bf16)

    lines, rings = [], []
    for i, (start, width, y_first, _) in enumerate(STREAMS):
        here, there, peers = (z, y, y_peers) if y_first else (y, z, z_peers)
        bufs[i][here, there] = pair[:, start : start + width]
        part = bufs[i].at[here, there]
        lines.append([remote(part, part, line_sems[i], 0, peers[d]) for d in range(NY - 1)])
    for d in (3, 2, 4, 1, 5, 0, 6):
        for line in lines:
            line[d].start()

    counts = jnp.where(first, counts_ref[0:1, :], counts_ref[1:2, :]).astype(f32)
    counts = jnp.broadcast_to(counts, (8, 128)).astype(bf16)
    before = lax.broadcasted_iota(jnp.int32, (128, 128), 0) < lax.broadcasted_iota(
        jnp.int32, (128, 128), 1
    )
    offsets = mm_nn(counts, before.astype(bf16)).astype(bf16)
    owner_row = lax.broadcasted_iota(jnp.int32, (128, 1024), 0)
    column = lax.broadcasted_iota(jnp.int32, (128, 1024), 1)
    slot = (lax.broadcasted_iota(jnp.int32, (8, 1024), 1) % MAXP).astype(f32)
    pivot_row = lax.broadcasted_iota(jnp.int32, (BLOCK, 1024), 0)

    def places(owner_of):
        spread = (owner_row == owner_of(column // MAXP)).astype(bf16)
        start, count = mm_nn(offsets, spread), mm_nn(counts, spread)
        target = jnp.where(slot < count, start + slot, -1.0)
        return (pivot_row.astype(f32) == target[0:1, :]).astype(bf16)

    def swapped(position):
        return ((position // CORES) % NZ * NY + position // (CORES * NZ)) * CORES + position % CORES

    compact = (places(swapped), places(lambda position: position))

    for i, (start, width, y_first, _) in enumerate(STREAMS):
        here, peers = (z, y_peers) if y_first else (y, z_peers)
        seven = bufs[i].at[here, pl.ds(0, NY - 1)]
        remote(seven, seven, line_sems[i], 0, peers[0]).wait()

    def ring(buf, sems, me, count, up, down):
        last = count // 2 - 1
        size = buf.shape[1] // PARTS

        def go_up(step, part, origin):
            piece = buf.at[origin % count, pl.ds(part * size, size)]
            return remote(piece, piece, sems, step * PARTS + part, up)

        def go_down(step, part, origin):
            piece = buf.at[origin % count, pl.ds(part * size, size)]
            return remote(piece, piece, sems, RECEIVED // 2 + step * PARTS + part - (step == last) * PARTS // 2, down)

        goes_up = lambda step, part: step < last or part < PARTS // 2
        goes_down = lambda step, part: step < last or part >= PARTS // 2

        def send(step, part):
            if goes_up(step, part):
                go_up(step, part, me + count - step).start()
            if goes_down(step, part):
                go_down(step, part, me + step).start()

        def receive(step, part):
            if goes_up(step, part):
                go_up(step, part, me + count - 1 - step).wait_recv()
            if goes_down(step, part):
                go_down(step, part, me + 1 + step).wait_recv()

        def finish():
            sent = buf.at[pl.ds(0, count - 1)]
            remote(sent, sent, sems, 0, up).wait_send()

        return send, receive, finish

    for i, (start, width, y_first, _) in enumerate(STREAMS):
        me, peers = (z, z_peers) if y_first else (y, y_peers)
        rings.append(ring(bufs[i], ring_sems[i], me, NZ, peers[0], peers[NZ - 2]))

    def go(i, step):
        for part in range(PARTS):
            if step:
                rings[i][1](step - 1, part)
            if step < NZ // 2:
                rings[i][0](step, part)

    half = BLOCK // 2
    def part(i, origin, at, count=half):
        place = STREAMS[i][3](origin)
        return g_ref.at[core, pl.ds(at * half, count), lanes(place, STREAMS[i][1])]

    def to_right(i, origin, at, index):
        return remote(part(i, origin, at), part(i, origin, at), x_sems[i], index, right)

    def to_left(i, origin, at, index):
        return remote(part(i, origin, at), part(i, origin, at), x_sems[i], 3 + index, left)

    def to_sibling(i, origin, index):
        block = part(i, origin, 0, BLOCK)
        return remote(block, block, k_sems[i], 0, sibling)

    def join(i):
        width, y_first = STREAMS[i][1:3]
        rows = bufs[i][...].reshape(1024, width)
        placed = mm_nn(compact[int(y_first)], rows).astype(bf16)
        g_ref[core, :, lanes(STREAMS[i][3](x), width)] = placed
        to_right(i, x, 0, 0).start()
        to_left(i, x, 1, 0).start()
        to_right(i, x, 1, 1).start()
        to_left(i, x, 0, 1).start()
        to_sibling(i, x, 0).start()

    def forward():
        for i in range(len(STREAMS)):
            to_right(i, x_left, 0, 0).wait_recv()
            to_right(i, x_left, 0, 2).start()
            to_left(i, x_right, 1, 0).wait_recv()
            to_left(i, x_right, 1, 2).start()

    def collect():
        for i in range(len(STREAMS)):
            to_right(i, x_left, 1, 1).wait_recv()
            to_sibling(i, x_left, 1).start()
            to_left(i, x_right, 0, 1).wait_recv()
            to_sibling(i, x_right, 2).start()

    def close():
        for i in range(len(STREAMS)):
            to_right(i, x_far, 0, 2).wait_recv()
            to_left(i, x_far, 1, 2).wait_recv()
            to_sibling(i, x_far, 3).start()

    for step in range(NZ // 2 + 1):
        for i in range(len(STREAMS)):
            go(i, step)
            if step == NZ // 2:
                join(i)
        if step == 2:
            share(0, x_right, 0, ROWS, left).wait_recv()
            share(2, x_right, 0, half_rows, left).start()
            share(1, x_left, 0, ROWS, right).wait_recv()
            share(3, x_left, half_rows, half_rows, right).start()
    forward()
    collect()
    close()
    for i, (start, width, y_first, _) in enumerate(STREAMS):
        rings[i][2]()
        three = g_ref.at[core, :, lanes(0, 3 * width)]
        remote(three, three, x_sems[i], 0, right).wait_send()
        four = g_ref.at[core, :, lanes(0, 4 * width)]
        remote(four, four, k_sems[i], 0, sibling).wait()
    share(2, x_far, 0, half_rows, left).wait_recv()
    share(3, x_far, half_rows, half_rows, right).wait_recv()
    share(0, x, 0, ROWS, left).wait_send()
    share(1, x, 0, ROWS, right).wait_send()
    share(2, x_right, 0, half_rows, left).wait_send()
    share(3, x_left, half_rows, half_rows, right).wait_send()


def gather_pivots(slots, counts, points, factor):
    vmem = pl.BlockSpec(memory_space=pltpu.VMEM)
    hbm = pl.BlockSpec(memory_space=pltpu.HBM)
    sems = lambda count: pltpu.SemaphoreType.DMA((1 + count,))
    each = len(STREAMS)
    return pl.pallas_call(
        gather_kernel,
        in_specs=[hbm] * 4,
        out_specs=[vmem, hbm],
        out_shape=(
            jax.ShapeDtypeStruct((2, BLOCK, NX * W), bf16),
            jax.ShapeDtypeStruct((ROWS, F), bf16),
        ),
        scratch_shapes=[
            pltpu.VMEM((ROWS, FQ), bf16),
            pltpu.VMEM((ROWS, KQ), bf16),
            pltpu.VMEM((2 * MAXP, W), bf16),
            pltpu.VMEM((2 * MAXP, W), bf16),
            pltpu.SemaphoreType.DMA((4,)),
            sems(1),
            *[sems(1)] * 4,
            pltpu.VMEM((2, MAXP), jnp.int32),
            pltpu.VMEM((2, 128), jnp.int32),
            *[pltpu.VMEM((NZ, NY, 2 * MAXP, stream[1]), bf16) for stream in STREAMS],
            *[sems(1)] * each,
            *[sems(RECEIVED)] * each,
            *[sems(6)] * each,
            *[sems(1)] * each,
        ],
        compiler_params=pltpu.CompilerParams(
            collective_id=0, has_side_effects=True, vmem_limit_bytes=60 * 2**20
        ),
        name="pivot_gather",
    )(slots, counts, points, factor)


def sum_kernel(
    coef_ref, out_ref, mine_coef, load_sem, got, total, rounded, got_z, piece, got_y, final, core_sem, z_sem, y_sem,
):
    z, y, core = spot()
    sibling = row_id(z, y, 1 - core)
    z_peers = [row_id((z + d) % NZ, y, core) for d in range(1, NZ)]
    y_same = [row_id(z, (y + d) % NY, core) for d in range(1, NY)]
    y_other = [row_id(z, (y + d) % NY, 1 - core) for d in range(NY)]
    wait_entered = enter(z_peers + y_same + y_other)
    load = pltpu.make_async_copy(coef_ref.at[core], mine_coef, load_sem)
    load.start()
    load.wait()
    wait_entered()

    swap = remote(coef_ref.at[1 - core], got, core_sem, 0, sibling)
    swap.start()
    swap.wait()
    total[...] = (mine_coef[...] + got[...]).reshape(NZ, 32, 128)
    rounded[...] = total[...].astype(bf16)
    for d in (3, 2, 4, 1, 5, 0, 6):
        remote(rounded.at[(z + d + 1) % NZ], got_z.at[d], z_sem, 0, z_peers[d]).start()
    remote(rounded.at[pl.ds(0, NZ - 1)], got_z, z_sem, 0, z_peers[0]).wait()
    mine = total[z]
    for d in range(NZ - 1):
        mine = mine + got_z[d].astype(f32)
    piece[...] = mine.reshape(4, 8, 128)
    for d in (4, 3, 5, 2, 6, 1, 7, 0):
        tile = piece.at[(y + d) % NY // 2]
        if d:
            remote(tile, got_y.at[core, d], y_sem, 0, y_same[d - 1]).start()
        remote(tile, got_y.at[core, d], y_sem, 1, y_other[d]).start()
    same, cross = got_y.at[core, pl.ds(1, NY - 1)], got_y.at[1 - core]
    remote(same, same, y_sem, 0, y_same[0]).wait()
    remote(cross, cross, y_sem, 1, y_other[0]).wait()
    got_y[core, 0] = piece[y // 2]
    for b in range(2):
        mine = got_y[b, 0]
        for d in range(1, NY):
            mine = mine + got_y[b, d]
        final[b] = mine
    at = (y % 2) * 4 + core * 2
    out_ref[0] = final[0, pl.ds(at, 2), :]
    out_ref[1] = final[1, pl.ds(at, 2), :]


def sum_coefficients(coef):
    vmem = pl.BlockSpec(memory_space=pltpu.VMEM)
    sems = lambda count: pltpu.SemaphoreType.DMA((1 + count,))
    return pl.pallas_call(
        sum_kernel,
        in_specs=[pl.BlockSpec(memory_space=pl.ANY)],
        out_specs=vmem,
        out_shape=jax.ShapeDtypeStruct((2, 2, 128), f32),
        scratch_shapes=[
            pltpu.VMEM((BLOCK, 128), f32),
            pltpu.SemaphoreType.DMA,
            pltpu.VMEM((BLOCK, 128), f32),
            pltpu.VMEM((NZ, 32, 128), f32),
            pltpu.VMEM((NZ, 32, 128), bf16),
            pltpu.VMEM((NZ - 1, 32, 128), bf16),
            pltpu.VMEM((4, 8, 128), f32),
            pltpu.VMEM((2, NY, 8, 128), f32),
            pltpu.VMEM((2, 8, 128), f32),
            sems(1),
            sems(1),
            sems(2),
        ],
        compiler_params=pltpu.CompilerParams(
            collective_id=1, has_side_effects=True, vmem_limit_bytes=63 * 2**20 + 2**19
        ),
        name="coefficient_sum",
    )(coef)


def local(points, factor, targets, pivot_slots, pivot_counts):
    g, x = gather_pivots(pivot_slots, pivot_counts, points, factor)
    new, res, coef = solve_rows(g, points, x, factor, targets)
    return jnp.swapaxes(new, 1, 2), res, sum_coefficients(coef)


def solution(mesh):
    in_specs = (P("rows", "cols"), P("rows", None), P("rows", "cols"), P(None, "rows"), P())
    out_specs = (P(None, "rows", "cols"), P(None, "rows"), P(None, "rows", "cols"))
    return jax.shard_map(local, mesh=mesh, in_specs=in_specs, out_specs=out_specs, check_vma=False)
```
